512 devices in a mesh: seq: 64 (over z, x, y_lo), fsdp: 8 (over y_hi, core).
Axes of the slice: x: 4, y: 8 (y_hi: 4, y_lo: 2; y = y_hi * 2 + y_lo), z: 8, core: 2. Of those that a mesh axis runs over, the one named last changes fastest.
Arguments:
- queries: bfloat16 [8192, 1024], P('seq', 'fsdp'), may hold values from -8 to 8
- keys: bfloat16 [8192, 1024], P('seq', 'fsdp'), may hold values from -8 to 8
- values: bfloat16 [8192, 1024], P('seq', 'fsdp'), may hold values from -12 to 12
- residual: bfloat16 [8192, 3072], P('seq', 'fsdp'), may hold values from -6 to 6
- gate: float32 [3072], replicated, may hold values from 0.25 to 2
- w_out: bfloat16 [1024, 3072], P('fsdp', 'seq'), may hold values from -0.1875 to 0.1875
- grad_out: bfloat16 [8192, 3072], P('seq'), may hold values from -6 to 6
- group_mask: int32 [128, 128], replicated, may hold values from 0 to 1, as said below
- group_of_slot: int32 [128], replicated, may hold values from 0 to 127, each once
Outputs:
- layer_out: bfloat16 [8192, 3072], P('seq', 'fsdp')
- d_queries: bfloat16 [8192, 1024], P('seq', 'fsdp')
- d_keys: bfloat16 [8192, 1024], P('seq', 'fsdp')
- d_values: bfloat16 [8192, 1024], P('seq', 'fsdp')
- d_weight: float32 [1024, 3072], P('fsdp', 'seq')
The draws below stay inside these ranges and needn't reach their ends.
Inputs may be any that keep to these rules, and one draw needn't show every extreme that they name: group_mask[i, j] is 1 where j equals i and 0 where j exceeds i. `group_of_slot`: each group stands in exactly one slot.
All inputs are finite; a program needn't handle non-finite values.
Results may differ from the reference program's by a relative error of at most 0.035.
Values may be sent and summed in bfloat16 or wider, within the bound.
No kernel may reach another device: no remote copies, remote signals or barrier semaphores. Data moves between devices by JAX's collectives and lax.ppermute only.
A program may use at most 64 MiB of HBM per device.

```python
import jax
import jax.numpy as jnp
from jax import lax

D = 3072
HEADS = 16
HD = 64
GROUP = 64
NGROUP = 128
TOKENS = 8192


def draw_queries(key, part):
    key = jax.random.fold_in(key, 11)
    base_draw = jnp.clip(1.4 * jax.random.normal(key, (TOKENS, HEADS * HD), jnp.float32), -8.0, 8.0)
    return base_draw.astype(jnp.bfloat16)


def draw_keys(key, part):
    key = jax.random.fold_in(key, 12)
    base_draw = jnp.clip(1.4 * jax.random.normal(key, (TOKENS, HEADS * HD), jnp.float32), -8.0, 8.0)
    return base_draw.astype(jnp.bfloat16)


def draw_group_mask(key, part):
    key = jax.random.fold_in(key, 21)
    coin_flip = jax.random.randint(key, (NGROUP, NGROUP), 0, 4)
    row_ids = jnp.arange(NGROUP)[:, None]
    col_ids = jnp.arange(NGROUP)[None, :]
    earlier = jnp.logical_and(col_ids < row_ids, coin_flip > 0)
    return jnp.where(jnp.logical_or(col_ids == row_ids, earlier), 1, 0).astype(jnp.int32)


def block_scale(stream_key, extent, shards, low, high):
    gain = 1.0
    for axis_at, shards_of in shards:
        heights = jax.random.uniform(jax.random.fold_in(jax.random.fold_in(stream_key, 6), axis_at), (shards_of,), jnp.float32, low / len(shards), high / len(shards))
        gain = gain * jnp.repeat(jnp.exp(heights), extent[axis_at] // shards_of).reshape((-1,) + (1,) * (len(extent) - 1 - axis_at))
    return gain


def centred(key, extent, scale, limit, cuts=(), kind=jnp.bfloat16):
    level = block_scale(key, extent, cuts, -0.22, 0.18) if cuts else 1.0
    values = jax.random.normal(key, extent, jnp.float32) * scale * level
    return jnp.minimum(jnp.maximum(values, -limit), limit).astype(kind)


def setup_inputs(seed: int = 0) -> dict:
    seeds = jax.random.split(jax.random.key(seed), 10)
    queries = draw_queries(jax.random.fold_in(seeds[9], 71), 0)
    keys = draw_keys(jax.random.fold_in(seeds[9], 71), 0)
    values = centred(seeds[2], (TOKENS, HEADS * HD), 2.0, 12.0, ((0, 64), (1, 8)))
    residual = centred(seeds[3], (TOKENS, D), 1.0, 6.0, ((0, 64), (1, 8)))
    gate = jnp.clip(jax.random.uniform(seeds[4], (D,), jnp.float32, 0.25, 2.0), 0.25, 2.0)
    w_out = centred(seeds[5], (HEADS * HD, D), (HEADS * HD) ** -0.5, 0.1875, ((0, 8), (1, 64)))
    grad_out = centred(seeds[6], (TOKENS, D), 1.0, 6.0, ((0, 64),))
    group_mask = draw_group_mask(jax.random.fold_in(seeds[9], 71), 0)
    group_of_slot = jax.random.permutation(seeds[8], NGROUP).astype(jnp.int32)
    return dict(queries=queries, keys=keys, values=values, residual=residual, gate=gate, w_out=w_out, grad_out=grad_out, group_mask=group_mask, group_of_slot=group_of_slot)


def reference(queries, keys, values, residual, gate, w_out, grad_out, group_mask, group_of_slot):
    score_scale = HD ** -0.5
    slot_ids = jnp.arange(TOKENS, dtype=jnp.int32) // GROUP
    group_ids = jnp.take(group_of_slot, slot_ids)
    allowed = jnp.take(jnp.take(group_mask, group_ids, axis=0), group_ids, axis=1) == 1
    gated_grad = (grad_out.astype(jnp.float32) * gate[None, :]).astype(jnp.bfloat16)
    d_attended = jnp.dot(gated_grad, w_out.T, preferred_element_type=jnp.float32).astype(jnp.bfloat16)

    def one_head(head_id):
        first_col = head_id * HD
        query_head = lax.dynamic_slice_in_dim(queries, first_col, HD, 1)
        key_head = lax.dynamic_slice_in_dim(keys, first_col, HD, 1)
        value_head = lax.dynamic_slice_in_dim(values, first_col, HD, 1)
        grad_head = lax.dynamic_slice_in_dim(d_attended, first_col, HD, 1)
        scores = jnp.dot(query_head, key_head.T, preferred_element_type=jnp.float32) * score_scale
        scores = jnp.where(allowed, scores, -jnp.inf)
        row_top = jnp.max(scores, axis=1, keepdims=True)
        log_total = row_top + jnp.log(jnp.sum(jnp.exp(scores - row_top), axis=1, keepdims=True))
        probability = jnp.exp(scores - log_total)
        weights = probability.astype(jnp.bfloat16)
        head_out = jnp.dot(weights, value_head, preferred_element_type=jnp.float32).astype(jnp.bfloat16)
        row_delta = jnp.sum(grad_head.astype(jnp.float32) * head_out.astype(jnp.float32), axis=1, keepdims=True)
        d_probs = jnp.dot(grad_head, value_head.T, preferred_element_type=jnp.float32)
        d_scores = (probability * (d_probs - row_delta)).astype(jnp.bfloat16)
        d_query = (jnp.dot(d_scores, key_head, preferred_element_type=jnp.float32) * score_scale).astype(jnp.bfloat16)
        d_key = (jnp.dot(d_scores.T, query_head, preferred_element_type=jnp.float32) * score_scale).astype(jnp.bfloat16)
        d_value = jnp.dot(weights.T, grad_head, preferred_element_type=jnp.float32).astype(jnp.bfloat16)
        return head_out, d_query, d_key, d_value

    head_ids = jnp.arange(HEADS, dtype=jnp.int32)
    head_out, d_query, d_key, d_value = lax.map(one_head, head_ids)

    def join_heads(stacked):
        return jnp.transpose(stacked, (1, 0, 2)).reshape(TOKENS, HEADS * HD)

    attended = join_heads(head_out)
    branch = jnp.dot(attended, w_out, preferred_element_type=jnp.float32)
    layer_out = (residual.astype(jnp.float32) + gate[None, :] * branch).astype(jnp.bfloat16)
    d_weight = jnp.dot(attended.T, gated_grad, preferred_element_type=jnp.float32)
    return layer_out, join_heads(d_query), join_heads(d_key), join_heads(d_value), d_weight
```

```python
import jax
import jax.numpy as jnp
from jax import lax
from jax.experimental import pallas as pl
from jax.experimental.pallas import tpu as pltpu
from jax.sharding import Mesh, PartitionSpec as P

ROW = ("x", "yl")
COL = ("z",)
FSDP = ("yh", "core")
SIDE = 8
TOK = 128
BLOCK = SIDE * TOK
FEAT = 128
HEADS_HERE = 2
HD = 64
GROUP = 64
GROUPS = BLOCK // GROUP
SHARD = 48
STRIP = SIDE * SHARD
TILE = 256
MASKED = -1e30
STATS = HEADS_HERE * SIDE
VMEM = 32 * 1024 * 1024
BF = jnp.bfloat16
F32 = jnp.float32


def mm(a, b):
    return jnp.dot(a, b, preferred_element_type=F32)


def call(body, out_shape, in_specs, flops=0, data=0, exps=0, **kw):
    return pl.pallas_call(
        body,
        grid=(1,),
        in_specs=in_specs,
        out_specs=jax.tree.map(lambda s: whole(s.shape), out_shape),
        out_shape=out_shape,
        compiler_params=pltpu.CompilerParams(vmem_limit_bytes=VMEM),
        cost_estimate=pl.CostEstimate(flops=flops, bytes_accessed=data, transcendentals=exps),
        **kw,
    )


def whole(shape):
    return pl.BlockSpec(shape, lambda i: (0,) * len(shape))


def at(shape, index):
    return pl.BlockSpec(shape, lambda i: index)


def out(shape, dtype=BF):
    return jax.ShapeDtypeStruct(shape, dtype)


def swap(a, axes):
    return lax.all_to_all(a, axes, 0, 0, tiled=True)


def first_payload(k_ref, v_ref, w_ref, o_ref):
    w_t = w_ref[...].astype(F32).T.astype(BF)
    for i in range(SIDE):
        o_ref[i, 0:TOK] = k_ref[...]
        o_ref[i, TOK : 2 * TOK] = v_ref[...]
        o_ref[i, 2 * TOK : 2 * TOK + SHARD] = w_t


def second_payload(g_ref, q_ref, o_ref):
    for i in range(SIDE):
        for j in range(SIDE):
            o_ref[i, j * SHARD : (j + 1) * SHARD] = g_ref[j, 2 * TOK : 2 * TOK + SHARD]
        o_ref[i, STRIP : STRIP + TOK] = q_ref[...]


def grad_payload(gated_ref, w_ref, o_ref):
    total = jnp.zeros((TOK, FEAT), F32)
    for i in range(SIDE):
        total = total + mm(gated_ref[:, i * STRIP : (i + 1) * STRIP], w_ref[i])
    grad_t = total.T.astype(BF)
    for i in range(SIDE):
        o_ref[i] = grad_t


def key_operand(k):
    row = lax.broadcasted_iota(jnp.int32, (BLOCK, GROUPS), 0) // GROUP
    col = lax.broadcasted_iota(jnp.int32, (BLOCK, GROUPS), 1)
    return jnp.concatenate([k, (row == col).astype(F32).astype(BF)], axis=1)


def query_operand(q_t, bias, head):
    mine = lax.broadcasted_iota(jnp.int32, (FEAT, 1), 0) // HD == head
    part = jnp.where(mine, q_t.astype(F32) * HD ** (-0.5), 0.0).astype(BF)
    return jnp.concatenate([part, bias], axis=0)


def transposed(a):
    return a.astype(F32).T.astype(BF)


def forward(q_ref, k_ref, v_ref, bias_ref, o_ref, lse_ref):
    q_t = transposed(q_ref[...].reshape(BLOCK, FEAT))
    k_op = key_operand(k_ref[...].reshape(BLOCK, FEAT))
    v_t = transposed(v_ref[...].reshape(BLOCK, FEAT))
    for head in range(HEADS_HERE):
        q_op = query_operand(q_t, bias_ref[...], head)
        for tile in range(BLOCK // TILE):
            span = slice(tile * TILE, (tile + 1) * TILE)
            s = mm(k_op, q_op[:, span])
            top = jnp.max(s, axis=0, keepdims=True)
            p = jnp.exp(s - top)
            total = jnp.sum(p, axis=0, keepdims=True)
            part = mm(v_t[head * HD : (head + 1) * HD], p.astype(BF))
            o_ref[head * HD : (head + 1) * HD, span] = part / total
            lse = top + jnp.log(total)
            for c in range(TILE // TOK):
                row = head * SIDE + tile * (TILE // TOK) + c
                lse_ref[row : row + 1, :] = lse[:, c * TOK : (c + 1) * TOK]


def split3(a):
    hi = a.astype(BF)
    rest = a - hi.astype(F32)
    mid = rest.astype(BF)
    return hi, mid, (rest - mid.astype(F32)).astype(BF)


def stats_payload(o_ref, lse_ref, grad_ref, out_ref):
    rows = [None] * STATS
    for c in range(SIDE):
        part = o_ref[:, c * TOK : (c + 1) * TOK]
        product = part * grad_ref[c].astype(F32)
        for head in range(HEADS_HERE):
            rows[head * SIDE + c] = jnp.sum(
                product[head * HD : (head + 1) * HD], axis=0, keepdims=True
            )
        out_ref[c, 0:FEAT] = part.astype(BF)
    pieces = jnp.concatenate(
        split3(lse_ref[...]) + split3(jnp.concatenate(rows, axis=0)), axis=0
    )
    for c in range(SIDE):
        out_ref[c, FEAT : FEAT + 6 * STATS] = pieces


def combine(me_ref, d_ref, lse_ref, delta_ref, att_ref, weight_ref):
    def quantity(j, first):
        at_row = FEAT + first * STATS
        return sum(
            d_ref[j, at_row + i * STATS : at_row + (i + 1) * STATS].astype(F32) for i in range(3)
        )

    lse = [quantity(j, 0) for j in range(SIDE)]
    top = lse[0]
    for j in range(1, SIDE):
        top = jnp.maximum(top, lse[j])
    total = jnp.zeros_like(top)
    for j in range(SIDE):
        total = total + jnp.exp(lse[j] - top)
    all_lse = top + jnp.log(total)
    lse_ref[...] = all_lse
    delta = jnp.zeros_like(top)
    for j in range(SIDE):
        weight = jnp.exp(lse[j] - all_lse)
        weight_ref[j] = weight
        delta = delta + weight * quantity(j, 3)
    delta_ref[...] = delta
    me = me_ref[0]
    heads = []
    for head in range(HEADS_HERE):
        acc = jnp.zeros((HD, TOK), F32)
        for j in range(SIDE):
            weight = weight_ref[j, pl.ds(head * SIDE + me, 1), :]
            acc = acc + weight * d_ref[j, head * HD : (head + 1) * HD].astype(F32)
        heads.append(acc)
    att_ref[...] = jnp.concatenate(heads, axis=0).T.astype(BF)


def backward(
    q_ref, k_ref, v_ref, grad_ref, bias_ref, lse_ref, delta_ref, att_ref, gated_ref,
    e_ref, f_ref, dk_ref, dv_ref,
):
    q = q_ref[...].reshape(BLOCK, FEAT)
    k = k_ref[...].reshape(BLOCK, FEAT)
    v = v_ref[...].reshape(BLOCK, FEAT)
    q_t = transposed(q)
    k_t = transposed(k)
    k_op = key_operand(k)
    grad_t = jnp.concatenate([grad_ref[c] for c in range(SIDE)], axis=1)
    grad = transposed(grad_t)
    feat_row = lax.broadcasted_iota(jnp.int32, (FEAT, 1), 0) // HD
    feat_col = lax.broadcasted_iota(jnp.int32, (1, FEAT), 1) // HD
    dk_ref[...] = jnp.zeros_like(dk_ref)
    dv_ref[...] = jnp.zeros_like(dv_ref)
    for head in range(HEADS_HERE):
        q_op = query_operand(q_t, bias_ref[...], head)
        grad_op = jnp.where(feat_row == head, grad_t.astype(F32), 0.0).astype(BF)
        q_rows = jnp.where(feat_col == head, q.astype(F32), 0.0).astype(BF)
        grad_rows = jnp.where(feat_col == head, grad.astype(F32), 0.0).astype(BF)
        for tile in range(BLOCK // TILE):
            span = slice(tile * TILE, (tile + 1) * TILE)
            first = head * SIDE + tile * (TILE // TOK)
            lse = jnp.concatenate(
                [lse_ref[first + c : first + c + 1, :] for c in range(TILE // TOK)], axis=1
            )
            delta = jnp.concatenate(
                [delta_ref[first + c : first + c + 1, :] for c in range(TILE // TOK)], axis=1
            )
            p = jnp.exp(mm(k_op, q_op[:, span]) - lse)
            ds = (p * (mm(v, grad_op[:, span]) - delta)).astype(BF)
            dq_t = mm(k_t[head * HD : (head + 1) * HD], ds).astype(BF)
            for c in range(TILE // TOK):
                to = STRIP + head * HD
                e_ref[tile * (TILE // TOK) + c, to : to + HD] = dq_t[:, c * TOK : (c + 1) * TOK]
            dv_ref[...] += mm(p.astype(BF), grad_rows[span])
            dk_ref[...] += mm(ds, q_rows[span])
    for i in range(SIDE):
        span = slice(i * TOK, (i + 1) * TOK)
        f_ref[i, 0:TOK] = (dk_ref[span] * HD ** (-0.5)).astype(BF)
        f_ref[i, TOK : 2 * TOK] = dv_ref[span].astype(BF)
        f_ref[i, 2 * TOK : 2 * TOK + SHARD] = jnp.zeros((SHARD, FEAT), BF)
    att = att_ref[...]
    for i in range(SIDE):
        e_ref[i, 0:STRIP] = mm(gated_ref[i * STRIP : (i + 1) * STRIP], att).astype(BF)


def sum_first(e_ref, dq_ref, f_ref):
    total = e_ref[0].astype(F32)
    for i in range(1, SIDE):
        total = total + e_ref[i].astype(F32)
    dq_ref[...] = (total[STRIP:].T * HD ** (-0.5)).astype(BF)
    shards = total[:STRIP].astype(BF)
    for i in range(SIDE):
        f_ref[i] = shards[i * SHARD : (i + 1) * SHARD]


def sum_second(f_ref, dk_ref, dv_ref, dw_ref):
    total = f_ref[0].astype(F32)
    for i in range(1, SIDE):
        total = total + f_ref[i].astype(F32)
    dk_ref[...] = total[0:TOK].astype(BF)
    dv_ref[...] = total[TOK : 2 * TOK].astype(BF)
    dw_ref[...] = total[2 * TOK : 2 * TOK + SHARD].T


def local(queries, keys, values, residual, gate, w_out, grad_out, group_mask, group_of_slot):
    z = lax.axis_index(COL)
    p = lax.axis_index(ROW)

    own = whole((TOK, FEAT))
    col_spec = whole((SIDE, 2 * TOK + SHARD, FEAT))
    row_spec = whole((SIDE, STRIP + TOK, FEAT))
    sent = call(
        first_payload,
        out((SIDE, 2 * TOK + SHARD, FEAT)),
        [own, own, whole((FEAT, SHARD))],
        data=1 << 20,
    )(keys, values, w_out)
    kvw = swap(sent, COL)

    slots = group_of_slot.reshape(SIDE, SIDE, TOK // GROUP)
    query_groups = lax.dynamic_index_in_dim(slots, z, 0, keepdims=False).reshape(GROUPS)
    key_groups = lax.dynamic_index_in_dim(slots, p, 1, keepdims=False).reshape(GROUPS)
    ids = jnp.arange(group_mask.shape[0], dtype=jnp.int32)
    query_hot = (query_groups[:, None] == ids[None, :]).astype(BF)
    key_hot = (key_groups[:, None] == ids[None, :]).astype(BF)
    picked = jnp.einsum(
        "qa,ab->bq", query_hot, (group_mask == 1).astype(BF), preferred_element_type=F32
    ).astype(BF)
    table = jnp.einsum("kb,bq->kq", key_hot, picked, preferred_element_type=F32)
    bias = jnp.where(table > 0.5, 0.0, MASKED).astype(BF)
    bias = jnp.broadcast_to(bias[:, :, None], (GROUPS, GROUPS, GROUP)).reshape(GROUPS, BLOCK)

    gated = (grad_out.astype(F32) * gate[None, :]).astype(BF)
    gated = gated.reshape(TOK, SIDE, SIDE, SHARD).transpose(0, 2, 1, 3).reshape(TOK, SIDE * STRIP)
    gated_t = gated.T

    sent = call(
        second_payload,
        out((SIDE, STRIP + TOK, FEAT)),
        [col_spec, own],
        data=2 << 20,
    )(kvw, queries)
    wq = swap(sent, ROW)

    sent = call(
        grad_payload,
        out((SIDE, FEAT, TOK)),
        [whole((TOK, SIDE * STRIP)), at((SIDE, STRIP, FEAT), (0, 0, 0))],
        flops=2 * TOK * FEAT * SIDE * STRIP,
        data=2 << 20,
    )(gated, wq)
    grad_t = swap(sent, ROW)

    query_spec = at((SIDE, TOK, FEAT), (0, STRIP // TOK, 0))
    key_spec = at((SIDE, TOK, FEAT), (0, 0, 0))
    value_spec = at((SIDE, TOK, FEAT), (0, 1, 0))
    bias_spec = whole((GROUPS, BLOCK))
    stat_spec = whole((STATS, TOK))
    pair_count = HEADS_HERE * BLOCK * BLOCK
    part, part_lse = call(
        forward,
        (out((FEAT, BLOCK), F32), out((STATS, TOK), F32)),
        [query_spec, key_spec, value_spec, bias_spec],
        flops=16 * HD * pair_count,
        data=2 << 20,
        exps=pair_count,
    )(wq, kvw, kvw, bias)
    sent = call(
        stats_payload,
        out((SIDE, FEAT + 6 * STATS, TOK)),
        [whole((FEAT, BLOCK)), stat_spec, whole((SIDE, FEAT, TOK))],
        data=2 << 20,
    )(part, part_lse, grad_t)
    parts = swap(sent, ROW)

    w_rows = (
        wq[:, :STRIP]
        .reshape(SIDE, SIDE, SHARD, FEAT)
        .transpose(1, 0, 2, 3)
        .reshape(SIDE * STRIP, FEAT)
    )
    lse, delta, attended = call(
        combine,
        (out((STATS, TOK), F32), out((STATS, TOK), F32), out((TOK, FEAT))),
        [pl.BlockSpec(memory_space=pltpu.SMEM), whole((SIDE, FEAT + 6 * STATS, TOK))],
        data=1 << 20,
        scratch_shapes=[pltpu.VMEM((SIDE, STATS, TOK), F32)],
    )(p.reshape(1).astype(jnp.int32), parts)
    branch = jnp.einsum("dk,tk->dt", w_rows, attended, preferred_element_type=F32).astype(BF)
    summed = lax.psum_scatter(branch, FSDP, scatter_dimension=0, tiled=True)

    sent_row, sent_col = call(
        backward,
        (out((SIDE, STRIP + TOK, FEAT)), out((SIDE, 2 * TOK + SHARD, FEAT))),
        [
            query_spec,
            key_spec,
            value_spec,
            whole((SIDE, FEAT, TOK)),
            bias_spec,
            stat_spec,
            stat_spec,
            whole((TOK, FEAT)),
            whole((SIDE * STRIP, TOK)),
        ],
        flops=40 * HD * pair_count,
        data=5 << 20,
        exps=pair_count,
        scratch_shapes=[pltpu.VMEM((BLOCK, FEAT), F32)] * 2,
    )(wq, kvw, kvw, grad_t, bias, lse, delta, attended, gated_t)
    got_row = swap(sent_row, ROW)
    d_queries, shards = call(
        sum_first,
        (out((TOK, FEAT)), out((SIDE, SHARD, FEAT))),
        [row_spec],
        data=2 << 20,
    )(got_row)
    sent_col = jnp.concatenate([sent_col[:, : 2 * TOK], shards], axis=1)
    got_col = swap(sent_col, COL)
    d_keys, d_values, d_weight = call(
        sum_second,
        (out((TOK, FEAT)), out((TOK, FEAT)), out((FEAT, SHARD), F32)),
        [col_spec],
        data=1 << 20,
    )(got_col)

    col_count = residual.shape[1]
    gate_here = lax.dynamic_slice_in_dim(gate, lax.axis_index(FSDP) * col_count, col_count, 0)
    layer_out = (
        residual.astype(F32) + gate_here[None, :] * summed.astype(F32).T
    ).astype(BF)
    return (layer_out, d_queries, d_keys, d_values, d_weight)


def solution(mesh):
    fine = Mesh(mesh.devices.reshape(8, 4, 2, 4, 2), ("z", "x", "yl", "yh", "core"))
    seq = COL + ROW
    tile = P(seq, FSDP)
    in_specs = (tile, tile, tile, tile, P(), P(FSDP, seq), P(seq, None), P(), P())
    out_specs = (tile, tile, tile, tile, P(FSDP, seq))
    return jax.shard_map(local, mesh=fine, in_specs=in_specs, out_specs=out_specs, check_vma=False)
```

```python
import jax
import jax.numpy as jnp
from jax import lax
from jax.experimental import pallas as pl
from jax.experimental.pallas import tpu as pltpu
from jax.sharding import Mesh, PartitionSpec as P

ROW = ("x", "yl")
COL = ("z",)
FSDP = ("yh", "core")
SIDE = 8
PAIRS = 4
TOK = 128
BLOCK = SIDE * TOK
FEAT = 128
HEADS_HERE = 2
HD = 64
GROUP = 64
GROUPS = BLOCK // GROUP
SHARD = 48
STRIP = SIDE * SHARD
TILE = 256
MASKED = -1e30
STATS = HEADS_HERE * SIDE
VMEM = 32 * 1024 * 1024
BF = jnp.bfloat16
F32 = jnp.float32


def mm(a, b):
    return jnp.dot(a, b, preferred_element_type=F32)


def call(body, out_shape, in_specs, flops=1, data=1, exps=0, out_specs=None, grid=(1,), **kw):
    if out_specs is None:
        out_specs = jax.tree.map(lambda s: whole(s.shape), out_shape)
    return pl.pallas_call(
        body,
        grid=grid,
        in_specs=in_specs,
        out_specs=out_specs,
        out_shape=out_shape,
        compiler_params=pltpu.CompilerParams(vmem_limit_bytes=VMEM),
        cost_estimate=pl.CostEstimate(flops=flops, bytes_accessed=data, transcendentals=exps),
        **kw,
    )


def hbm(*arrays):
    return [pltpu.with_memory_space_constraint(a, pltpu.HBM) for a in arrays]


def whole(shape):
    return pl.BlockSpec(shape, lambda i: (0,) * len(shape))


def at(shape, index):
    return pl.BlockSpec(shape, lambda i: index)


def out(shape, dtype=BF):
    return jax.ShapeDtypeStruct(shape, dtype)


def far(shape, dtype=BF):
    return pltpu.HBM(shape, dtype)


def swap(a, axes):
    return lax.all_to_all(a, axes, 0, 0, tiled=True)


def repeat(block_ref, o_ref, sems):
    copies = [pltpu.make_async_copy(block_ref, o_ref.at[i], sems.at[i]) for i in range(SIDE)]
    for copy in copies:
        copy.start()
    for copy in copies:
        copy.wait()


def first_payload(k_ref, v_ref, w_ref, o_ref, block_ref, sems):
    block_ref[0:TOK] = k_ref[...]
    block_ref[TOK : 2 * TOK] = v_ref[...]
    block_ref[2 * TOK : 2 * TOK + SHARD] = w_ref[...]
    repeat(block_ref, o_ref, sems)


def second_payload(g_ref, q_ref, o_ref, block_ref, sems):
    for j in range(SIDE):
        block_ref[j * SHARD : (j + 1) * SHARD] = g_ref[j, 2 * TOK : 2 * TOK + SHARD]
    block_ref[STRIP : STRIP + TOK] = q_ref[...]
    repeat(block_ref, o_ref, sems)


def grad_payload(gated_ref, w_ref, o_ref, block_ref, sems):
    total = jnp.zeros((TOK, FEAT), F32)
    for i in range(SIDE):
        total = total + mm(gated_ref[:, i * STRIP : (i + 1) * STRIP], w_ref[i])
    block_ref[...] = total.T.astype(BF)
    repeat(block_ref, o_ref, sems)


def key_operand(k):
    row = lax.broadcasted_iota(jnp.int32, (BLOCK, GROUPS), 0) // GROUP
    col = lax.broadcasted_iota(jnp.int32, (BLOCK, GROUPS), 1)
    return jnp.concatenate([k, (row == col).astype(F32).astype(BF)], axis=1)


def query_operand(q_t, bias, head):
    mine = lax.broadcasted_iota(jnp.int32, (FEAT, 1), 0) // HD == head
    part = jnp.where(mine, q_t.astype(F32) * HD ** (-0.5), 0.0).astype(BF)
    return jnp.concatenate([part, bias], axis=0)


def transposed(a):
    return a.astype(F32).T.astype(BF)


def row_of(ref, head, tile):
    first = head * SIDE + tile * (TILE // TOK)
    return jnp.concatenate([ref[first + c : first + c + 1, :] for c in range(TILE // TOK)], axis=1)


def forward(q_ref, k_ref, v_ref, bias_ref, o_ref, mean_ref, lse_ref):
    q_t = transposed(q_ref[...].reshape(BLOCK, FEAT))
    k = k_ref[...].reshape(BLOCK, FEAT)
    k_op = key_operand(k)
    k_t = transposed(k)
    v_t = transposed(v_ref[...].reshape(BLOCK, FEAT))
    for head in range(HEADS_HERE):
        rows = slice(head * HD, (head + 1) * HD)
        q_op = query_operand(q_t, bias_ref[...], head)
        both = jnp.concatenate([v_t[rows], k_t[rows]], axis=0)
        for tile in range(BLOCK // TILE):
            span = slice(tile * TILE, (tile + 1) * TILE)
            s = mm(k_op, q_op[:, span])
            top = jnp.max(s, axis=0, keepdims=True)
            p = jnp.exp(s - top)
            total = jnp.sum(p, axis=0, keepdims=True)
            part = mm(both, p.astype(BF)) * (1.0 / total)
            o_ref[rows, span] = part[:HD].astype(BF)
            mean_ref[rows, span] = part[HD:].astype(BF)
            lse = top + jnp.log(total)
            for c in range(TILE // TOK):
                row = head * SIDE + tile * (TILE // TOK) + c
                lse_ref[row : row + 1, :] = lse[:, c * TOK : (c + 1) * TOK]


def split3(a):
    hi = a.astype(BF)
    rest = a - hi.astype(F32)
    mid = rest.astype(BF)
    return hi, mid, (rest - mid.astype(F32)).astype(BF)


def stats_payload(o_ref, lse_ref, grad_ref, out_ref, delta_ref):
    for c in range(SIDE):
        part = o_ref[:, c * TOK : (c + 1) * TOK]
        product = part.astype(F32) * grad_ref[c].astype(F32)
        for head in range(HEADS_HERE):
            row = head * SIDE + c
            delta_ref[row : row + 1, :] = jnp.sum(
                product[head * HD : (head + 1) * HD], axis=0, keepdims=True
            )
        out_ref[c, 0:FEAT] = part
    pieces = jnp.concatenate(split3(lse_ref[...]) + split3(delta_ref[...]), axis=0)
    for c in range(SIDE):
        out_ref[c, FEAT : FEAT + 6 * STATS] = pieces


def query_grad(q_ref, k_ref, v_ref, grad_ref, bias_ref, lse_ref, delta_ref, o_ref):
    k = k_ref[...].reshape(BLOCK, FEAT)
    v = v_ref[...].reshape(BLOCK, FEAT)
    q_t = transposed(q_ref[...].reshape(BLOCK, FEAT))
    k_t = transposed(k)
    k_op = key_operand(k)
    grad_t = jnp.concatenate([grad_ref[c] for c in range(SIDE)], axis=1)
    feat_row = lax.broadcasted_iota(jnp.int32, (FEAT, 1), 0) // HD
    for head in range(HEADS_HERE):
        rows = slice(head * HD, (head + 1) * HD)
        q_op = query_operand(q_t, bias_ref[...], head)
        grad_op = jnp.where(feat_row == head, grad_t.astype(F32), 0.0).astype(BF)
        for tile in range(BLOCK // TILE):
            span = slice(tile * TILE, (tile + 1) * TILE)
            p = jnp.exp(mm(k_op, q_op[:, span]) - row_of(lse_ref, head, tile))
            ds = (p * (mm(v, grad_op[:, span]) - row_of(delta_ref, head, tile))).astype(BF)
            o_ref[rows, span] = mm(k_t[rows], ds).astype(BF)


def combine(me_ref, d_ref, lse_ref, delta_ref, att_ref, weight_ref):
    def quantity(j, first):
        at_row = FEAT + first * STATS
        return sum(
            d_ref[j, at_row + i * STATS : at_row + (i + 1) * STATS].astype(F32) for i in range(3)
        )

    lse = [quantity(j, 0) for j in range(SIDE)]
    top = lse[0]
    for j in range(1, SIDE):
        top = jnp.maximum(top, lse[j])
    total = jnp.zeros_like(top)
    for j in range(SIDE):
        total = total + jnp.exp(lse[j] - top)
    all_lse = top + jnp.log(total)
    lse_ref[...] = all_lse
    delta = jnp.zeros_like(top)
    for j in range(SIDE):
        weight = jnp.exp(lse[j] - all_lse)
        weight_ref[j] = weight
        delta = delta + weight * quantity(j, 3)
    delta_ref[...] = delta
    me = me_ref[0]
    heads = []
    for head in range(HEADS_HERE):
        acc = jnp.zeros((HD, TOK), F32)
        for j in range(SIDE):
            weight = weight_ref[j, pl.ds(head * SIDE + me, 1), :]
            acc = acc + weight * d_ref[j, head * HD : (head + 1) * HD].astype(F32)
        heads.append(acc)
    att_ref[...] = jnp.concatenate(heads, axis=0).T.astype(BF)


def branch_rows(core_ref, att_ref, w_ref, keep_ref, send_ref, all_ref):
    att = att_ref[...]
    for i in range(SIDE):
        part = lax.dot_general(
            w_ref[i], att, (((1,), (1,)), ((), ())), preferred_element_type=F32
        ).astype(BF)
        for j in range(SIDE):
            all_ref[j, i * SHARD : (i + 1) * SHARD] = part[j * SHARD : (j + 1) * SHARD]
    core = core_ref[0]
    for i in range(PAIRS):
        keep_ref[i] = all_ref[2 * i + core]
        send_ref[i] = all_ref[2 * i + 1 - core]


def add_halves(pair_ref, keep_ref, got_ref, *out_refs):
    for d, o_ref in enumerate(out_refs):
        i = lax.rem(pair_ref[0] + d, PAIRS)
        o_ref[...] = (keep_ref[i].astype(F32) + got_ref[i].astype(F32)).astype(BF)


def row_payload(
    grad_ref, mean_ref, lse_ref, delta_ref, all_lse_ref, all_delta_ref, att_ref, gated_ref, e_ref
):
    att = att_ref[...]
    for i in range(SIDE):
        cols = slice(i * TOK, (i + 1) * TOK)
        for head in range(HEADS_HERE):
            rows = slice(head * HD, (head + 1) * HD)
            row = slice(head * SIDE + i, head * SIDE + i + 1)
            weight = jnp.exp(lse_ref[row, :] - all_lse_ref[row, :])
            shift = all_delta_ref[row, :] - delta_ref[row, :]
            part = grad_ref[rows, cols].astype(F32) - shift * mean_ref[rows, cols].astype(F32)
            e_ref[i, STRIP + head * HD : STRIP + (head + 1) * HD] = (weight * part).astype(BF)
        e_ref[i, 0:STRIP] = mm(gated_ref[i * STRIP : (i + 1) * STRIP], att).astype(BF)


def key_grads(
    q_ref, k_ref, v_ref, grad_ref, bias_ref, lse_ref, delta_ref, f_ref, dk_ref, dv_ref
):
    q = q_ref[...].reshape(BLOCK, FEAT)
    k = k_ref[...].reshape(BLOCK, FEAT)
    v = v_ref[...].reshape(BLOCK, FEAT)
    q_t = transposed(q)
    k_op = key_operand(k)
    grad_t = jnp.concatenate([grad_ref[c] for c in range(SIDE)], axis=1)
    grad = transposed(grad_t)
    feat_row = lax.broadcasted_iota(jnp.int32, (FEAT, 1), 0) // HD
    feat_col = lax.broadcasted_iota(jnp.int32, (1, FEAT), 1) // HD
    dk_ref[...] = jnp.zeros_like(dk_ref)
    dv_ref[...] = jnp.zeros_like(dv_ref)
    for head in range(HEADS_HERE):
        q_op = query_operand(q_t, bias_ref[...], head)
        grad_op = jnp.where(feat_row == head, grad_t.astype(F32), 0.0).astype(BF)
        q_rows = jnp.where(feat_col == head, q.astype(F32), 0.0).astype(BF)
        grad_rows = jnp.where(feat_col == head, grad.astype(F32), 0.0).astype(BF)
        for tile in range(BLOCK // TILE):
            span = slice(tile * TILE, (tile + 1) * TILE)
            p = jnp.exp(mm(k_op, q_op[:, span]) - row_of(lse_ref, head, tile))
            ds = (p * (mm(v, grad_op[:, span]) - row_of(delta_ref, head, tile))).astype(BF)
            dv_ref[...] += mm(p.astype(BF), grad_rows[span])
            dk_ref[...] += mm(ds, q_rows[span])
    for i in range(SIDE):
        span = slice(i * TOK, (i + 1) * TOK)
        f_ref[i, 0:TOK] = (dk_ref[span] * HD ** (-0.5)).astype(BF)
        f_ref[i, TOK : 2 * TOK] = dv_ref[span].astype(BF)
        f_ref[i, 2 * TOK : 2 * TOK + SHARD] = jnp.zeros((SHARD, FEAT), BF)


def sum_first(e_ref, f_in, dq_ref, f_ref, shard_ref, sem):
    del f_in
    total = e_ref[0].astype(F32)
    for i in range(1, SIDE):
        total = total + e_ref[i].astype(F32)
    shards = total[:STRIP].astype(BF)
    for i in range(SIDE):
        shard_ref[i] = shards[i * SHARD : (i + 1) * SHARD]
    copy = pltpu.make_async_copy(shard_ref, f_ref.at[:, 2 * TOK : 2 * TOK + SHARD], sem)
    copy.start()
    dq_ref[...] = (total[STRIP:].T * HD ** (-0.5)).astype(BF)
    copy.wait()


def sum_second(f_ref, dk_ref, dv_ref, dw_ref):
    total = f_ref[0].astype(F32)
    for i in range(1, SIDE):
        total = total + f_ref[i].astype(F32)
    dk_ref[...] = total[0:TOK].astype(BF)
    dv_ref[...] = total[TOK : 2 * TOK].astype(BF)
    dw_ref[...] = total[2 * TOK : 2 * TOK + SHARD]


def finish(residual_ref, gate_ref, *refs):
    total = refs[0][...].astype(F32)
    for ref in refs[1:-1]:
        total = total + ref[...].astype(F32)
    refs[-1][...] = (residual_ref[...].astype(F32) + gate_ref[...] * total.T).astype(BF)


def local(queries, keys, values, residual, gate, w_out, grad_out, group_mask, group_of_slot):
    z = lax.axis_index(COL)
    p = lax.axis_index(ROW)
    anywhere = pl.BlockSpec(memory_space=pl.ANY)

    def scratch(rows):
        return [pltpu.VMEM((rows, FEAT), BF), pltpu.SemaphoreType.DMA((SIDE,))]

    own = whole((TOK, FEAT))
    col_spec = whole((SIDE, 2 * TOK + SHARD, FEAT))
    row_spec = whole((SIDE, STRIP + TOK, FEAT))
    sent = call(
        first_payload,
        far((SIDE, 2 * TOK + SHARD, FEAT)),
        [own, own, whole((SHARD, FEAT))],
        data=1 << 20,
        out_specs=anywhere,
        scratch_shapes=scratch(2 * TOK + SHARD),
    )(*hbm(keys, values, w_out.T))
    kvw = swap(sent, COL)

    slots = group_of_slot.reshape(SIDE, SIDE, TOK // GROUP)
    query_groups = lax.dynamic_index_in_dim(slots, z, 0, keepdims=False).reshape(GROUPS)
    key_groups = lax.dynamic_index_in_dim(slots, p, 1, keepdims=False).reshape(GROUPS)
    ids = jnp.arange(group_mask.shape[0], dtype=jnp.int32)
    query_hot = (query_groups[:, None] == ids[None, :]).astype(BF)
    key_hot = (key_groups[:, None] == ids[None, :]).astype(BF)
    picked = jnp.einsum(
        "qa,ab->bq", query_hot, (group_mask == 1).astype(BF), preferred_element_type=F32
    ).astype(BF)
    table = jnp.einsum("kb,bq->kq", key_hot, picked, preferred_element_type=F32)
    bias = jnp.where(table > 0.5, 0.0, MASKED).astype(BF)
    bias = jnp.broadcast_to(bias[:, :, None], (GROUPS, GROUPS, GROUP)).reshape(GROUPS, BLOCK)

    gated = (grad_out.astype(F32) * gate[None, :]).astype(BF)
    gated = gated.reshape(TOK, SIDE, SIDE, SHARD).transpose(0, 2, 1, 3).reshape(TOK, SIDE * STRIP)
    gated_t = gated.T

    sent = call(
        second_payload,
        far((SIDE, STRIP + TOK, FEAT)),
        [col_spec, own],
        data=2 << 20,
        out_specs=anywhere,
        scratch_shapes=scratch(STRIP + TOK),
    )(kvw, queries)
    wq = swap(sent, ROW)

    sent = call(
        grad_payload,
        far((SIDE, FEAT, TOK)),
        [whole((TOK, SIDE * STRIP)), at((SIDE, STRIP, FEAT), (0, 0, 0))],
        flops=2 * TOK * FEAT * SIDE * STRIP,
        data=2 << 20,
        out_specs=anywhere,
        scratch_shapes=scratch(FEAT),
    )(gated, wq)
    grad_t = swap(sent, ROW)

    query_spec = at((SIDE, TOK, FEAT), (0, STRIP // TOK, 0))
    key_spec = at((SIDE, TOK, FEAT), (0, 0, 0))
    value_spec = at((SIDE, TOK, FEAT), (0, 1, 0))
    bias_spec = whole((GROUPS, BLOCK))
    stat_spec = whole((STATS, TOK))
    pair_count = HEADS_HERE * BLOCK * BLOCK
    half_spec = whole((FEAT, BLOCK))
    part, mean_key, part_lse = call(
        forward,
        (far((FEAT, BLOCK)), far((FEAT, BLOCK)), out((STATS, TOK), F32)),
        [query_spec, key_spec, value_spec, bias_spec],
        flops=24 * HD * pair_count,
        data=2 << 20,
        exps=pair_count,
    )(wq, kvw, kvw, bias)
    sent, part_delta = call(
        stats_payload,
        (far((SIDE, FEAT + 6 * STATS, TOK)), out((STATS, TOK), F32)),
        [half_spec, stat_spec, whole((SIDE, FEAT, TOK))],
        data=2 << 20,
    )(*hbm(part), part_lse, grad_t)
    parts = swap(sent, ROW)
    block_specs = [
        query_spec,
        key_spec,
        value_spec,
        whole((SIDE, FEAT, TOK)),
        bias_spec,
        stat_spec,
        stat_spec,
    ]
    query_share = call(
        query_grad,
        far((FEAT, BLOCK)),
        block_specs,
        flops=24 * HD * pair_count,
        data=3 << 20,
        exps=pair_count,
    )(wq, kvw, kvw, grad_t, bias, part_lse, part_delta)

    parts, query_share = lax.optimization_barrier((parts, query_share))
    lse, delta, attended = call(
        combine,
        (out((STATS, TOK), F32), out((STATS, TOK), F32), out((TOK, FEAT))),
        [pl.BlockSpec(memory_space=pltpu.SMEM), whole((SIDE, FEAT + 6 * STATS, TOK))],
        data=1 << 20,
        scratch_shapes=[pltpu.VMEM((SIDE, STATS, TOK), F32)],
    )(p.reshape(1).astype(jnp.int32), parts)
    scalar = pl.BlockSpec(memory_space=pltpu.SMEM)
    core = lax.axis_index("core").reshape(1).astype(jnp.int32)
    pair = lax.axis_index("yh").reshape(1).astype(jnp.int32)
    keep, send = call(
        branch_rows,
        (out((PAIRS, STRIP, TOK)), out((PAIRS, STRIP, TOK))),
        [scalar, own, at((SIDE, STRIP, FEAT), (0, 0, 0))],
        flops=2 * TOK * FEAT * SIDE * STRIP,
        data=2 << 20,
        scratch_shapes=[pltpu.VMEM((SIDE, STRIP, TOK), BF)],
    )(core, attended, wq)
    got = lax.ppermute(send, "core", [(0, 1), (1, 0)])
    chunks = call(
        add_halves,
        (out((STRIP, TOK)),) * PAIRS,
        [scalar] + [whole((PAIRS, STRIP, TOK))] * 2,
        data=2 << 20,
    )(pair, keep, got)

    sent_row = call(
        row_payload,
        far((SIDE, STRIP + TOK, FEAT)),
        [half_spec, half_spec] + [stat_spec] * 4 + [own, whole((SIDE * STRIP, TOK))],
        flops=2 * TOK * FEAT * SIDE * STRIP,
        data=3 << 20,
    )(*hbm(query_share, mean_key), part_lse, part_delta, lse, delta, attended, gated_t)
    got_row = swap(sent_row, ROW)
    got_row, chunks = lax.optimization_barrier((got_row, chunks))
    summed = [chunks[0]] + [
        lax.ppermute(chunks[d], "yh", [(i, (i + d) % PAIRS) for i in range(PAIRS)])
        for d in range(1, PAIRS)
    ]
    col_shape = (SIDE, 2 * TOK + SHARD, FEAT)
    sent_col = call(
        key_grads,
        far(col_shape),
        block_specs,
        flops=32 * HD * pair_count,
        data=3 << 20,
        exps=pair_count,
        scratch_shapes=[pltpu.VMEM((BLOCK, FEAT), F32)] * 2,
    )(wq, kvw, kvw, grad_t, bias, lse, delta)
    d_queries, sent_col = call(
        sum_first,
        (out((TOK, FEAT)), far(col_shape)),
        [row_spec, anywhere],
        data=2 << 20,
        out_specs=(own, anywhere),
        input_output_aliases={1: 1},
        scratch_shapes=[pltpu.VMEM((SIDE, SHARD, FEAT), BF), pltpu.SemaphoreType.DMA],
    )(got_row, sent_col)
    got_col = swap(sent_col, COL)
    d_keys, d_values, d_weight = call(
        sum_second,
        (out((TOK, FEAT)), out((TOK, FEAT)), out((SHARD, FEAT), F32)),
        [col_spec],
        data=1 << 20,
    )(got_col)

    col_count = residual.shape[1]
    gate_here = lax.dynamic_slice_in_dim(gate, lax.axis_index(FSDP) * col_count, col_count, 0)
    layer_out = call(
        finish,
        out((TOK, STRIP)),
        [whole((TOK, STRIP)), whole((1, STRIP))] + [whole((STRIP, TOK))] * PAIRS,
        data=1 << 20,
    )(*hbm(residual), gate_here[None, :], *summed)
    return (layer_out, d_queries, d_keys, d_values, d_weight.T)


def solution(mesh):
    fine = Mesh(mesh.devices.reshape(8, 4, 2, 4, 2), ("z", "x", "yl", "yh", "core"))
    seq = COL + ROW
    tile = P(seq, FSDP)
    in_specs = (tile, tile, tile, tile, P(), P(FSDP, seq), P(seq, None), P(), P())
    out_specs = (tile, tile, tile, tile, P(FSDP, seq))
    return jax.shard_map(local, mesh=fine, in_specs=in_specs, out_specs=out_specs, check_vma=False)
```

```python
import jax
import jax.numpy as jnp
from jax import lax
from jax.experimental import pallas as pl
from jax.experimental.pallas import tpu as pltpu
from jax.sharding import Mesh, PartitionSpec as P

ROW = ("x", "yl")
COL = ("z",)
FSDP = ("yh", "core")
SIDE = 8
PAIRS = 4
TOK = 128
BLOCK = SIDE * TOK
FEAT = 128
HEADS_HERE = 2
HD = 64
GROUP = 64
GROUPS = BLOCK // GROUP
SHARD = 48
STRIP = SIDE * SHARD
QUERY_TILE = 512
KEY_TILE = 256
MASKED = -1e30
STATS = HEADS_HERE * SIDE
VMEM = 32 * 1024 * 1024
BF = jnp.bfloat16
F32 = jnp.float32


def mm(a, b):
    return jnp.dot(a, b, preferred_element_type=F32)


def call(body, out_shape, in_specs, flops=1, data=1, exps=0, out_specs=None, grid=(1,), **kw):
    if out_specs is None:
        out_specs = jax.tree.map(lambda s: whole(s.shape), out_shape)
    return pl.pallas_call(
        body,
        grid=grid,
        in_specs=in_specs,
        out_specs=out_specs,
        out_shape=out_shape,
        compiler_params=pltpu.CompilerParams(vmem_limit_bytes=VMEM),
        cost_estimate=pl.CostEstimate(flops=flops, bytes_accessed=data, transcendentals=exps),
        **kw,
    )


def hbm(*arrays):
    return [pltpu.with_memory_space_constraint(a, pltpu.HBM) for a in arrays]


def whole(shape):
    return pl.BlockSpec(shape, lambda i: (0,) * len(shape))


def at(shape, index):
    return pl.BlockSpec(shape, lambda i: index)


def out(shape, dtype=BF):
    return jax.ShapeDtypeStruct(shape, dtype)


def far(shape, dtype=BF):
    return pltpu.HBM(shape, dtype)


def swap(a, axes):
    return lax.all_to_all(a, axes, 0, 0, tiled=True)


def repeat(block_ref, o_ref, sems):
    copies = [pltpu.make_async_copy(block_ref, o_ref.at[i], sems.at[i]) for i in range(SIDE)]
    for copy in copies:
        copy.start()
    for copy in copies:
        copy.wait()


def first_payload(k_ref, v_ref, w_ref, o_ref, block_ref, sems):
    block_ref[0:TOK] = k_ref[...]
    block_ref[TOK : 2 * TOK] = v_ref[...]
    block_ref[2 * TOK : 2 * TOK + SHARD] = w_ref[...]
    repeat(block_ref, o_ref, sems)


def second_payload(g_ref, q_ref, o_ref, block_ref, sems):
    for j in range(SIDE):
        block_ref[j * SHARD : (j + 1) * SHARD] = g_ref[j, 2 * TOK : 2 * TOK + SHARD]
    block_ref[STRIP : STRIP + TOK] = q_ref[...]
    repeat(block_ref, o_ref, sems)


def grad_payload(gated_ref, w_ref, o_ref, block_ref, sems):
    total = jnp.zeros((TOK, FEAT), F32)
    for i in range(SIDE):
        total = total + mm(gated_ref[:, i * STRIP : (i + 1) * STRIP], w_ref[i])
    block_ref[...] = total.T.astype(BF)
    repeat(block_ref, o_ref, sems)


def key_operand(k):
    row = lax.broadcasted_iota(jnp.int32, (BLOCK, GROUPS), 0) // GROUP
    col = lax.broadcasted_iota(jnp.int32, (BLOCK, GROUPS), 1)
    return jnp.concatenate([k, (row == col).astype(F32).astype(BF)], axis=1)


def query_operand(q_t, bias, head):
    mine = lax.broadcasted_iota(jnp.int32, (FEAT, 1), 0) // HD == head
    part = jnp.where(mine, q_t.astype(F32) * HD ** (-0.5), 0.0).astype(BF)
    return jnp.concatenate([part, bias], axis=0)


def transposed(a):
    return a.astype(F32).T.astype(BF)


def row_of(ref, head, first=0, count=SIDE):
    rows = range(head * SIDE + first, head * SIDE + first + count)
    return jnp.concatenate([ref[i : i + 1, :] for i in rows], axis=1)


def forward(q_ref, k_ref, v_ref, bias_ref, o_ref, mean_ref, lse_ref):
    q_t = transposed(q_ref[...].reshape(BLOCK, FEAT))
    k = k_ref[...].reshape(BLOCK, FEAT)
    k_op = key_operand(k)
    k_t = transposed(k)
    v_t = transposed(v_ref[...].reshape(BLOCK, FEAT))
    for head in range(HEADS_HERE):
        rows = slice(head * HD, (head + 1) * HD)
        s = mm(k_op, query_operand(q_t, bias_ref[...], head))
        top = jnp.max(s, axis=0, keepdims=True)
        p = jnp.exp(s - top)
        total = jnp.sum(p, axis=0, keepdims=True)
        both = jnp.concatenate([v_t[rows], k_t[rows]], axis=0)
        part = mm(both, p.astype(BF)) * (1.0 / total)
        o_ref[rows] = part[:HD].astype(BF)
        mean_ref[rows] = part[HD:].astype(BF)
        lse = top + jnp.log(total)
        for c in range(SIDE):
            row = head * SIDE + c
            lse_ref[row : row + 1, :] = lse[:, c * TOK : (c + 1) * TOK]


def split3(a):
    hi = a.astype(BF)
    rest = a - hi.astype(F32)
    mid = rest.astype(BF)
    return hi, mid, (rest - mid.astype(F32)).astype(BF)


def stats_payload(o_ref, lse_ref, grad_ref, out_ref, delta_ref):
    for c in range(SIDE):
        part = o_ref[:, c * TOK : (c + 1) * TOK]
        product = part.astype(F32) * grad_ref[c].astype(F32)
        for head in range(HEADS_HERE):
            row = head * SIDE + c
            delta_ref[row : row + 1, :] = jnp.sum(
                product[head * HD : (head + 1) * HD], axis=0, keepdims=True
            )
        out_ref[c, 0:FEAT] = part
    pieces = jnp.concatenate(split3(lse_ref[...]) + split3(delta_ref[...]), axis=0)
    for c in range(SIDE):
        out_ref[c, FEAT : FEAT + 6 * STATS] = pieces


def query_grad(q_ref, k_ref, v_ref, grad_ref, bias_ref, lse_ref, delta_ref, o_ref):
    k = k_ref[...].reshape(BLOCK, FEAT)
    v = v_ref[...].reshape(BLOCK, FEAT)
    q_t = transposed(q_ref[...].reshape(BLOCK, FEAT))
    k_t = transposed(k)
    k_op = key_operand(k)
    grad_t = jnp.concatenate([grad_ref[c] for c in range(SIDE)], axis=1)
    feat_row = lax.broadcasted_iota(jnp.int32, (FEAT, 1), 0) // HD
    for head in range(HEADS_HERE):
        rows = slice(head * HD, (head + 1) * HD)
        q_op = query_operand(q_t, bias_ref[...], head)
        grad_op = jnp.where(feat_row == head, grad_t.astype(F32), 0.0).astype(BF)
        for tile in range(BLOCK // QUERY_TILE):
            span = slice(tile * QUERY_TILE, (tile + 1) * QUERY_TILE)
            part = (head, tile * (QUERY_TILE // TOK), QUERY_TILE // TOK)
            p = jnp.exp(mm(k_op, q_op[:, span]) - row_of(lse_ref, *part))
            ds = (p * (mm(v, grad_op[:, span]) - row_of(delta_ref, *part))).astype(BF)
            o_ref[rows, span] = mm(k_t[rows], ds).astype(BF)


def combine(me_ref, d_ref, lse_ref, delta_ref, att_ref, weight_ref):
    def quantity(j, first):
        at_row = FEAT + first * STATS
        return sum(
            d_ref[j, at_row + i * STATS : at_row + (i + 1) * STATS].astype(F32) for i in range(3)
        )

    lse = [quantity(j, 0) for j in range(SIDE)]
    top = lse[0]
    for j in range(1, SIDE):
        top = jnp.maximum(top, lse[j])
    total = jnp.zeros_like(top)
    for j in range(SIDE):
        total = total + jnp.exp(lse[j] - top)
    all_lse = top + jnp.log(total)
    lse_ref[...] = all_lse
    delta = jnp.zeros_like(top)
    for j in range(SIDE):
        weight = jnp.exp(lse[j] - all_lse)
        weight_ref[j] = weight
        delta = delta + weight * quantity(j, 3)
    delta_ref[...] = delta
    me = me_ref[0]
    heads = []
    for head in range(HEADS_HERE):
        acc = jnp.zeros((HD, TOK), F32)
        for j in range(SIDE):
            weight = weight_ref[j, pl.ds(head * SIDE + me, 1), :]
            acc = acc + weight * d_ref[j, head * HD : (head + 1) * HD].astype(F32)
        heads.append(acc)
    att_ref[...] = jnp.concatenate(heads, axis=0).T.astype(BF)


def branch_rows(place_ref, att_ref, w_ref, keep_ref, send_ref, all_ref):
    att = att_ref[...]
    for i in range(SIDE):
        part = lax.dot_general(
            w_ref[i], att, (((1,), (1,)), ((), ())), preferred_element_type=F32
        ).astype(BF)
        for j in range(SIDE):
            all_ref[j, i * SHARD : (i + 1) * SHARD] = part[j * SHARD : (j + 1) * SHARD]
    core = place_ref[1]
    for i in range(PAIRS):
        keep_ref[i] = all_ref[2 * i + core]
        send_ref[i] = all_ref[2 * i + 1 - core]


def add_halves(place_ref, keep_ref, got_ref, own_ref, far_ref, ahead_ref, behind_ref):
    pair, ahead = place_ref[0], 1 - 2 * place_ref[1]
    steps = ((own_ref, 0), (far_ref, 2), (ahead_ref, ahead), (behind_ref, -ahead))
    for ref, step in steps:
        i = lax.rem(pair + step + PAIRS, PAIRS)
        ref[...] = (keep_ref[i].astype(F32) + got_ref[i].astype(F32)).astype(BF)


def relay(ahead_ref, got_ref, o_ref):
    o_ref[...] = (ahead_ref[...].astype(F32) + got_ref[...].astype(F32)).astype(BF)


def row_payload(
    grad_ref, mean_ref, lse_ref, delta_ref, all_lse_ref, all_delta_ref, att_ref, gated_ref, o_ref,
    e_ref, sems,
):
    att = att_ref[...]
    copies = []
    for i in range(SIDE):
        cols = slice(i * TOK, (i + 1) * TOK)
        for head in range(HEADS_HERE):
            rows = slice(head * HD, (head + 1) * HD)
            row = slice(head * SIDE + i, head * SIDE + i + 1)
            weight = jnp.exp(lse_ref[row, :] - all_lse_ref[row, :])
            shift = all_delta_ref[row, :] - delta_ref[row, :]
            part = grad_ref[rows, cols].astype(F32) - shift * mean_ref[rows, cols].astype(F32)
            e_ref[i, STRIP + head * HD : STRIP + (head + 1) * HD] = (weight * part).astype(BF)
        e_ref[i, 0:STRIP] = mm(gated_ref[i * STRIP : (i + 1) * STRIP], att).astype(BF)
        copies.append(pltpu.make_async_copy(e_ref.at[i], o_ref.at[i], sems.at[i]))
        copies[i].start()
    for copy in copies:
        copy.wait()


def key_grads(
    q_ref, k_ref, v_ref, grad_ref, bias_ref, lse_ref, delta_ref, f_ref, dk_ref, dv_ref
):
    q = q_ref[...].reshape(BLOCK, FEAT)
    k = k_ref[...].reshape(BLOCK, FEAT)
    v = v_ref[...].reshape(BLOCK, FEAT)
    q_t = transposed(q)
    k_op = key_operand(k)
    grad_t = jnp.concatenate([grad_ref[c] for c in range(SIDE)], axis=1)
    grad = transposed(grad_t)
    feat_row = lax.broadcasted_iota(jnp.int32, (FEAT, 1), 0) // HD
    feat_col = lax.broadcasted_iota(jnp.int32, (1, FEAT), 1) // HD
    dk_ref[...] = jnp.zeros_like(dk_ref)
    dv_ref[...] = jnp.zeros_like(dv_ref)
    for head in range(HEADS_HERE):
        q_op = query_operand(q_t, bias_ref[...], head)
        grad_op = jnp.where(feat_row == head, grad_t.astype(F32), 0.0).astype(BF)
        q_rows = jnp.where(feat_col == head, q.astype(F32), 0.0).astype(BF)
        grad_rows = jnp.where(feat_col == head, grad.astype(F32), 0.0).astype(BF)
        for tile in range(BLOCK // KEY_TILE):
            span = slice(tile * KEY_TILE, (tile + 1) * KEY_TILE)
            part = (head, tile * (KEY_TILE // TOK), KEY_TILE // TOK)
            p = jnp.exp(mm(k_op, q_op[:, span]) - row_of(lse_ref, *part))
            ds = (p * (mm(v, grad_op[:, span]) - row_of(delta_ref, *part))).astype(BF)
            dv_ref[...] += mm(p.astype(BF), grad_rows[span])
            dk_ref[...] += mm(ds, q_rows[span])
    for i in range(SIDE):
        span = slice(i * TOK, (i + 1) * TOK)
        f_ref[i, 0:TOK] = (dk_ref[span] * HD ** (-0.5)).astype(BF)
        f_ref[i, TOK : 2 * TOK] = dv_ref[span].astype(BF)
        f_ref[i, 2 * TOK : 2 * TOK + SHARD] = jnp.zeros((SHARD, FEAT), BF)


def sum_first(e_ref, f_in, dq_ref, f_ref, shard_ref, sem):
    del f_in
    total = e_ref[0].astype(F32)
    for i in range(1, SIDE):
        total = total + e_ref[i].astype(F32)
    shards = total[:STRIP].astype(BF)
    for i in range(SIDE):
        shard_ref[i] = shards[i * SHARD : (i + 1) * SHARD]
    copy = pltpu.make_async_copy(shard_ref, f_ref.at[:, 2 * TOK : 2 * TOK + SHARD], sem)
    copy.start()
    dq_ref[...] = (total[STRIP:].T * HD ** (-0.5)).astype(BF)
    copy.wait()


def sum_second(f_ref, dk_ref, dv_ref, dw_ref):
    total = f_ref[0].astype(F32)
    for i in range(1, SIDE):
        total = total + f_ref[i].astype(F32)
    dk_ref[...] = total[0:TOK].astype(BF)
    dv_ref[...] = total[TOK : 2 * TOK].astype(BF)
    dw_ref[...] = total[2 * TOK : 2 * TOK + SHARD]


def finish(residual_ref, gate_ref, *refs):
    total = refs[0][...].astype(F32)
    for ref in refs[1:-1]:
        total = total + ref[...].astype(F32)
    refs[-1][...] = (residual_ref[...].astype(F32) + gate_ref[...] * total.T).astype(BF)


def local(queries, keys, values, residual, gate, w_out, grad_out, group_mask, group_of_slot):
    z = lax.axis_index(COL)
    p = lax.axis_index(ROW)
    anywhere = pl.BlockSpec(memory_space=pl.ANY)

    def scratch(rows):
        return [pltpu.VMEM((rows, FEAT), BF), pltpu.SemaphoreType.DMA((SIDE,))]

    own = whole((TOK, FEAT))
    col_spec = whole((SIDE, 2 * TOK + SHARD, FEAT))
    row_spec = whole((SIDE, STRIP + TOK, FEAT))
    sent = call(
        first_payload,
        far((SIDE, 2 * TOK + SHARD, FEAT)),
        [own, own, whole((SHARD, FEAT))],
        data=1 << 20,
        out_specs=anywhere,
        scratch_shapes=scratch(2 * TOK + SHARD),
    )(*hbm(keys, values, w_out.T))
    kvw = swap(sent, COL)

    slots = group_of_slot.reshape(SIDE, SIDE, TOK // GROUP)
    query_groups = lax.dynamic_index_in_dim(slots, z, 0, keepdims=False).reshape(GROUPS)
    key_groups = lax.dynamic_index_in_dim(slots, p, 1, keepdims=False).reshape(GROUPS)
    ids = jnp.arange(group_mask.shape[0], dtype=jnp.int32)
    query_hot = (query_groups[:, None] == ids[None, :]).astype(BF)
    key_hot = (key_groups[:, None] == ids[None, :]).astype(BF)
    picked = jnp.einsum(
        "qa,ab->bq", query_hot, (group_mask == 1).astype(BF), preferred_element_type=F32
    ).astype(BF)
    table = jnp.einsum("kb,bq->kq", key_hot, picked, preferred_element_type=F32)
    bias = jnp.where(table > 0.5, 0.0, MASKED).astype(BF)
    bias = jnp.broadcast_to(bias[:, :, None], (GROUPS, GROUPS, GROUP)).reshape(GROUPS, BLOCK)

    gated = (grad_out.astype(F32) * gate[None, :]).astype(BF)
    gated = gated.reshape(TOK, SIDE, SIDE, SHARD).transpose(0, 2, 1, 3).reshape(TOK, SIDE * STRIP)
    gated_t = gated.T

    sent = call(
        second_payload,
        far((SIDE, STRIP + TOK, FEAT)),
        [col_spec, own],
        data=2 << 20,
        out_specs=anywhere,
        scratch_shapes=scratch(STRIP + TOK),
    )(kvw, queries)
    wq = swap(sent, ROW)

    gated, wq, bias = lax.optimization_barrier((gated, wq, bias))
    sent = call(
        grad_payload,
        far((SIDE, FEAT, TOK)),
        [whole((TOK, SIDE * STRIP)), at((SIDE, STRIP, FEAT), (0, 0, 0))],
        flops=2 * TOK * FEAT * SIDE * STRIP,
        data=2 << 20,
        out_specs=anywhere,
        scratch_shapes=scratch(FEAT),
    )(gated, wq)
    grad_t = swap(sent, ROW)

    query_spec = at((SIDE, TOK, FEAT), (0, STRIP // TOK, 0))
    key_spec = at((SIDE, TOK, FEAT), (0, 0, 0))
    value_spec = at((SIDE, TOK, FEAT), (0, 1, 0))
    bias_spec = whole((GROUPS, BLOCK))
    stat_spec = whole((STATS, TOK))
    pair_count = HEADS_HERE * BLOCK * BLOCK
    half_spec = whole((FEAT, BLOCK))
    part, mean_key, part_lse = call(
        forward,
        (far((FEAT, BLOCK)), far((FEAT, BLOCK)), out((STATS, TOK), F32)),
        [query_spec, key_spec, value_spec, bias_spec],
        flops=24 * HD * pair_count,
        data=2 << 20,
        exps=pair_count,
    )(wq, kvw, kvw, bias)
    sent, part_delta = call(
        stats_payload,
        (far((SIDE, FEAT + 6 * STATS, TOK)), out((STATS, TOK), F32)),
        [half_spec, stat_spec, whole((SIDE, FEAT, TOK))],
        data=2 << 20,
    )(*hbm(part), part_lse, grad_t)
    parts = swap(sent, ROW)
    block_specs = [
        query_spec,
        key_spec,
        value_spec,
        whole((SIDE, FEAT, TOK)),
        bias_spec,
        stat_spec,
        stat_spec,
    ]
    query_share = call(
        query_grad,
        far((FEAT, BLOCK)),
        block_specs,
        flops=24 * HD * pair_count,
        data=3 << 20,
        exps=pair_count,
    )(wq, kvw, kvw, grad_t, bias, part_lse, part_delta)

    parts, query_share = lax.optimization_barrier((parts, query_share))
    lse, delta, attended = call(
        combine,
        (out((STATS, TOK), F32), out((STATS, TOK), F32), out((TOK, FEAT))),
        [pl.BlockSpec(memory_space=pltpu.SMEM), whole((SIDE, FEAT + 6 * STATS, TOK))],
        data=1 << 20,
        scratch_shapes=[pltpu.VMEM((SIDE, STATS, TOK), F32)],
    )(p.reshape(1).astype(jnp.int32), parts)
    scalar = pl.BlockSpec(memory_space=pltpu.SMEM)
    place = jnp.stack([lax.axis_index("yh"), lax.axis_index("core")]).astype(jnp.int32)
    keep, send = call(
        branch_rows,
        (out((PAIRS, STRIP, TOK)), out((PAIRS, STRIP, TOK))),
        [scalar, own, at((SIDE, STRIP, FEAT), (0, 0, 0))],
        flops=2 * TOK * FEAT * SIDE * STRIP,
        data=2 << 20,
        scratch_shapes=[pltpu.VMEM((SIDE, STRIP, TOK), BF)],
    )(place, attended, wq)
    got = lax.ppermute(send, "core", [(0, 1), (1, 0)])
    chunks = call(
        add_halves,
        (out((STRIP, TOK)),) * PAIRS,
        [scalar] + [whole((PAIRS, STRIP, TOK))] * 2,
        data=2 << 20,
    )(place, keep, got)

    sent_row = call(
        row_payload,
        far((SIDE, STRIP + TOK, FEAT)),
        [half_spec, half_spec] + [stat_spec] * 4 + [own, whole((SIDE * STRIP, TOK))],
        flops=2 * TOK * FEAT * SIDE * STRIP,
        data=3 << 20,
        out_specs=anywhere,
        scratch_shapes=[
            pltpu.VMEM((SIDE, STRIP + TOK, FEAT), BF),
            pltpu.SemaphoreType.DMA((SIDE,)),
        ],
    )(*hbm(query_share, mean_key), part_lse, part_delta, lse, delta, attended, gated_t)
    got_row = swap(sent_row, ROW)
    got_row, chunks = lax.optimization_barrier((got_row, chunks))
    mine, far_chunk, ahead_chunk, behind_chunk = chunks

    def pass_on(a, step):
        pairs = [
            (2 * i + c, 2 * ((i + step * (1 - 2 * c)) % PAIRS) + c)
            for i in range(PAIRS)
            for c in range(2)
        ]
        return lax.ppermute(a, FSDP, pairs)

    strip_spec = whole((STRIP, TOK))
    from_ahead = pass_on(behind_chunk, -1)
    ahead_chunk = call(relay, out((STRIP, TOK)), [strip_spec, strip_spec], data=1 << 18)(
        ahead_chunk, pass_on(far_chunk, 1)
    )
    summed = (mine, from_ahead, pass_on(ahead_chunk, 1))
    col_shape = (SIDE, 2 * TOK + SHARD, FEAT)
    sent_col = call(
        key_grads,
        far(col_shape),
        block_specs,
        flops=32 * HD * pair_count,
        data=3 << 20,
        exps=pair_count,
        scratch_shapes=[pltpu.VMEM((BLOCK, FEAT), F32)] * 2,
    )(wq, kvw, kvw, grad_t, bias, lse, delta)
    d_queries, sent_col = call(
        sum_first,
        (out((TOK, FEAT)), far(col_shape)),
        [row_spec, anywhere],
        data=2 << 20,
        out_specs=(own, anywhere),
        input_output_aliases={1: 1},
        scratch_shapes=[pltpu.VMEM((SIDE, SHARD, FEAT), BF), pltpu.SemaphoreType.DMA],
    )(got_row, sent_col)
    got_col = swap(sent_col, COL)
    d_keys, d_values, d_weight = call(
        sum_second,
        (out((TOK, FEAT)), out((TOK, FEAT)), out((SHARD, FEAT), F32)),
        [col_spec],
        data=1 << 20,
    )(got_col)

    col_count = residual.shape[1]
    gate_here = lax.dynamic_slice_in_dim(gate, lax.axis_index(FSDP) * col_count, col_count, 0)
    layer_out = call(
        finish,
        out((TOK, STRIP)),
        [whole((TOK, STRIP)), whole((1, STRIP))] + [strip_spec] * 3,
        data=1 << 20,
    )(residual, gate_here[None, :], *summed)
    return (layer_out, d_queries, d_keys, d_values, d_weight.T)


def solution(mesh):
    fine = Mesh(mesh.devices.reshape(8, 4, 2, 4, 2), ("z", "x", "yl", "yh", "core"))
    seq = COL + ROW
    tile = P(seq, FSDP)
    in_specs = (tile, tile, tile, tile, P(), P(FSDP, seq), P(seq, None), P(), P())
    out_specs = (tile, tile, tile, tile, P(FSDP, seq))
    return jax.shard_map(local, mesh=fine, in_specs=in_specs, out_specs=out_specs, check_vma=False)
```

```python
import jax
import jax.numpy as jnp
from jax import lax
from jax.experimental import pallas as pl
from jax.experimental.pallas import tpu as pltpu
from jax.sharding import Mesh, PartitionSpec as P

ROW = ("x", "yl")
COL = ("z",)
FSDP = ("yh", "core")
SIDE = 8
PAIRS = 4
TOK = 128
BLOCK = SIDE * TOK
FEAT = 128
HEADS_HERE = 2
HD = 64
GROUP = 64
GROUPS = BLOCK // GROUP
SHARD = 48
STRIP = SIDE * SHARD
QUERY_TILE = 512
KEY_TILE = 256
MASKED = -1e30
STATS = HEADS_HERE * SIDE
VMEM = 32 * 1024 * 1024
BF = jnp.bfloat16
F32 = jnp.float32


def mm(a, b):
    return jnp.dot(a, b, preferred_element_type=F32)


def call(body, out_shape, in_specs, flops=1, data=1, exps=0, out_specs=None, grid=(1,), **kw):
    if out_specs is None:
        out_specs = jax.tree.map(lambda s: whole(s.shape), out_shape)
    return pl.pallas_call(
        body,
        grid=grid,
        in_specs=in_specs,
        out_specs=out_specs,
        out_shape=out_shape,
        compiler_params=pltpu.CompilerParams(vmem_limit_bytes=VMEM),
        cost_estimate=pl.CostEstimate(flops=flops, bytes_accessed=data, transcendentals=exps),
        **kw,
    )


def hbm(*arrays):
    return [pltpu.with_memory_space_constraint(a, pltpu.HBM) for a in arrays]


def whole(shape):
    return pl.BlockSpec(shape, lambda i: (0,) * len(shape))


def at(shape, index):
    return pl.BlockSpec(shape, lambda i: index)


def out(shape, dtype=BF):
    return jax.ShapeDtypeStruct(shape, dtype)


def far(shape, dtype=BF):
    return pltpu.HBM(shape, dtype)


def swap(a, axes):
    return lax.all_to_all(a, axes, 0, 0, tiled=True)


def repeat(block_ref, o_ref, sems):
    copies = [pltpu.make_async_copy(block_ref, o_ref.at[i], sems.at[i]) for i in range(SIDE)]
    for copy in copies:
        copy.start()
    for copy in copies:
        copy.wait()


def first_payload(k_ref, v_ref, w_ref, o_ref):
    for i in range(SIDE):
        o_ref[i, 0:TOK] = k_ref[...]
        o_ref[i, TOK : 2 * TOK] = v_ref[...]
        o_ref[i, 2 * TOK : 2 * TOK + SHARD] = w_ref[...]


def second_payload(g_ref, q_ref, o_ref, block_ref, sems):
    for j in range(SIDE):
        block_ref[j * SHARD : (j + 1) * SHARD] = g_ref[j, 2 * TOK : 2 * TOK + SHARD]
    block_ref[STRIP : STRIP + TOK] = q_ref[...]
    repeat(block_ref, o_ref, sems)


def grad_payload(gated_ref, w_ref, o_ref, block_ref, sems):
    total = jnp.zeros((TOK, FEAT), F32)
    for i in range(SIDE):
        total = total + mm(gated_ref[:, i * STRIP : (i + 1) * STRIP], w_ref[i])
    block_ref[...] = total.T.astype(BF)
    repeat(block_ref, o_ref, sems)


def key_operand(k):
    row = lax.broadcasted_iota(jnp.int32, (BLOCK, GROUPS), 0) // GROUP
    col = lax.broadcasted_iota(jnp.int32, (BLOCK, GROUPS), 1)
    return jnp.concatenate([k, (row == col).astype(F32).astype(BF)], axis=1)


def query_operand(q_t, bias, head):
    mine = lax.broadcasted_iota(jnp.int32, (FEAT, 1), 0) // HD == head
    part = jnp.where(mine, q_t.astype(F32) * HD ** (-0.5), 0.0).astype(BF)
    return jnp.concatenate([part, bias], axis=0)


def transposed(a):
    return a.astype(F32).T.astype(BF)


def row_of(ref, head, first=0, count=SIDE):
    rows = range(head * SIDE + first, head * SIDE + first + count)
    return jnp.concatenate([ref[i : i + 1, :] for i in rows], axis=1)


def forward(q_ref, k_ref, v_ref, bias_ref, o_ref, mean_ref, lse_ref):
    q_t = transposed(q_ref[...].reshape(BLOCK, FEAT))
    k = k_ref[...].reshape(BLOCK, FEAT)
    k_op = key_operand(k)
    k_t = transposed(k)
    v_t = transposed(v_ref[...].reshape(BLOCK, FEAT))
    for head in range(HEADS_HERE):
        rows = slice(head * HD, (head + 1) * HD)
        s = mm(k_op, query_operand(q_t, bias_ref[...], head))
        top = jnp.max(s, axis=0, keepdims=True)
        p = jnp.exp(s - top)
        total = jnp.sum(p, axis=0, keepdims=True)
        both = jnp.concatenate([v_t[rows], k_t[rows]], axis=0)
        part = mm(both, p.astype(BF)) * (1.0 / total)
        o_ref[rows] = part[:HD].astype(BF)
        mean_ref[rows] = part[HD:].astype(BF)
        lse = top + jnp.log(total)
        for c in range(SIDE):
            row = head * SIDE + c
            lse_ref[row : row + 1, :] = lse[:, c * TOK : (c + 1) * TOK]


def split3(a):
    hi = a.astype(BF)
    rest = a - hi.astype(F32)
    mid = rest.astype(BF)
    return hi, mid, (rest - mid.astype(F32)).astype(BF)


def stats_payload(o_ref, lse_ref, grad_ref, out_ref, delta_ref):
    for c in range(SIDE):
        part = o_ref[:, c * TOK : (c + 1) * TOK]
        product = part.astype(F32) * grad_ref[c].astype(F32)
        for head in range(HEADS_HERE):
            row = head * SIDE + c
            delta_ref[row : row + 1, :] = jnp.sum(
                product[head * HD : (head + 1) * HD], axis=0, keepdims=True
            )
        out_ref[c, 0:FEAT] = part
    pieces = jnp.concatenate(split3(lse_ref[...]) + split3(delta_ref[...]), axis=0)
    for c in range(SIDE):
        out_ref[c, FEAT : FEAT + 6 * STATS] = pieces


def query_grad(q_ref, k_ref, v_ref, grad_ref, bias_ref, lse_ref, delta_ref, o_ref):
    k = k_ref[...].reshape(BLOCK, FEAT)
    v = v_ref[...].reshape(BLOCK, FEAT)
    q_t = transposed(q_ref[...].reshape(BLOCK, FEAT))
    k_t = transposed(k)
    k_op = key_operand(k)
    grad_t = jnp.concatenate([grad_ref[c] for c in range(SIDE)], axis=1)
    feat_row = lax.broadcasted_iota(jnp.int32, (FEAT, 1), 0) // HD
    for head in range(HEADS_HERE):
        rows = slice(head * HD, (head + 1) * HD)
        q_op = query_operand(q_t, bias_ref[...], head)
        grad_op = jnp.where(feat_row == head, grad_t.astype(F32), 0.0).astype(BF)
        for tile in range(BLOCK // QUERY_TILE):
            span = slice(tile * QUERY_TILE, (tile + 1) * QUERY_TILE)
            part = (head, tile * (QUERY_TILE // TOK), QUERY_TILE // TOK)
            p = jnp.exp(mm(k_op, q_op[:, span]) - row_of(lse_ref, *part))
            ds = (p * (mm(v, grad_op[:, span]) - row_of(delta_ref, *part))).astype(BF)
            o_ref[rows, span] = mm(k_t[rows], ds).astype(BF)


def combine(me_ref, d_ref, lse_ref, delta_ref, att_ref, weight_ref):
    def quantity(j, first):
        at_row = FEAT + first * STATS
        return sum(
            d_ref[j, at_row + i * STATS : at_row + (i + 1) * STATS].astype(F32) for i in range(3)
        )

    lse = [quantity(j, 0) for j in range(SIDE)]
    top = lse[0]
    for j in range(1, SIDE):
        top = jnp.maximum(top, lse[j])
    total = jnp.zeros_like(top)
    for j in range(SIDE):
        total = total + jnp.exp(lse[j] - top)
    all_lse = top + jnp.log(total)
    lse_ref[...] = all_lse
    delta = jnp.zeros_like(top)
    for j in range(SIDE):
        weight = jnp.exp(lse[j] - all_lse)
        weight_ref[j] = weight
        delta = delta + weight * quantity(j, 3)
    delta_ref[...] = delta
    me = me_ref[0]
    heads = []
    for head in range(HEADS_HERE):
        acc = jnp.zeros((HD, TOK), F32)
        for j in range(SIDE):
            weight = weight_ref[j, pl.ds(head * SIDE + me, 1), :]
            acc = acc + weight * d_ref[j, head * HD : (head + 1) * HD].astype(F32)
        heads.append(acc)
    att_ref[...] = jnp.concatenate(heads, axis=0).T.astype(BF)


def branch_rows(place_ref, att_ref, w_ref, keep_ref, send_ref, all_ref):
    att = att_ref[...]
    for i in range(SIDE):
        part = lax.dot_general(
            w_ref[i], att, (((1,), (1,)), ((), ())), preferred_element_type=F32
        ).astype(BF)
        for j in range(SIDE):
            all_ref[j, i * SHARD : (i + 1) * SHARD] = part[j * SHARD : (j + 1) * SHARD]
    core = place_ref[1]
    for i in range(PAIRS):
        keep_ref[i] = all_ref[2 * i + core]
        send_ref[i] = all_ref[2 * i + 1 - core]


def add_halves(place_ref, keep_ref, got_ref, own_ref, far_ref, ahead_ref, behind_ref):
    pair, ahead = place_ref[0], 1 - 2 * place_ref[1]
    steps = ((own_ref, 0), (far_ref, 2), (ahead_ref, ahead), (behind_ref, -ahead))
    for ref, step in steps:
        i = lax.rem(pair + step + PAIRS, PAIRS)
        ref[...] = (keep_ref[i].astype(F32) + got_ref[i].astype(F32)).astype(BF)


def relay(ahead_ref, got_ref, o_ref):
    o_ref[...] = (ahead_ref[...].astype(F32) + got_ref[...].astype(F32)).astype(BF)


def row_payload(
    grad_ref, mean_ref, lse_ref, delta_ref, all_lse_ref, all_delta_ref, att_ref, gated_ref, o_ref,
    e_ref, sems,
):
    att = att_ref[...]
    copies = []
    for i in range(SIDE):
        cols = slice(i * TOK, (i + 1) * TOK)
        for head in range(HEADS_HERE):
            rows = slice(head * HD, (head + 1) * HD)
            row = slice(head * SIDE + i, head * SIDE + i + 1)
            weight = jnp.exp(lse_ref[row, :] - all_lse_ref[row, :])
            shift = all_delta_ref[row, :] - delta_ref[row, :]
            part = grad_ref[rows, cols].astype(F32) - shift * mean_ref[rows, cols].astype(F32)
            e_ref[i, STRIP + head * HD : STRIP + (head + 1) * HD] = (weight * part).astype(BF)
        e_ref[i, 0:STRIP] = mm(gated_ref[i * STRIP : (i + 1) * STRIP], att).astype(BF)
        copies.append(pltpu.make_async_copy(e_ref.at[i], o_ref.at[i], sems.at[i]))
        copies[i].start()
    for copy in copies:
        copy.wait()


def key_grads(
    q_ref, k_ref, v_ref, grad_ref, bias_ref, lse_ref, delta_ref, f_ref, dk_ref, dv_ref
):
    q = q_ref[...].reshape(BLOCK, FEAT)
    k = k_ref[...].reshape(BLOCK, FEAT)
    v = v_ref[...].reshape(BLOCK, FEAT)
    q_t = transposed(q)
    k_op = key_operand(k)
    grad_t = jnp.concatenate([grad_ref[c] for c in range(SIDE)], axis=1)
    grad = transposed(grad_t)
    feat_row = lax.broadcasted_iota(jnp.int32, (FEAT, 1), 0) // HD
    feat_col = lax.broadcasted_iota(jnp.int32, (1, FEAT), 1) // HD
    dk_ref[...] = jnp.zeros_like(dk_ref)
    dv_ref[...] = jnp.zeros_like(dv_ref)
    for head in range(HEADS_HERE):
        q_op = query_operand(q_t, bias_ref[...], head)
        grad_op = jnp.where(feat_row == head, grad_t.astype(F32), 0.0).astype(BF)
        q_rows = jnp.where(feat_col == head, q.astype(F32), 0.0).astype(BF)
        grad_rows = jnp.where(feat_col == head, grad.astype(F32), 0.0).astype(BF)
        for tile in range(BLOCK // KEY_TILE):
            span = slice(tile * KEY_TILE, (tile + 1) * KEY_TILE)
            part = (head, tile * (KEY_TILE // TOK), KEY_TILE // TOK)
            p = jnp.exp(mm(k_op, q_op[:, span]) - row_of(lse_ref, *part))
            ds = (p * (mm(v, grad_op[:, span]) - row_of(delta_ref, *part))).astype(BF)
            dv_ref[...] += mm(p.astype(BF), grad_rows[span])
            dk_ref[...] += mm(ds, q_rows[span])
    for i in range(SIDE):
        span = slice(i * TOK, (i + 1) * TOK)
        f_ref[i, 0:TOK] = (dk_ref[span] * HD ** (-0.5)).astype(BF)
        f_ref[i, TOK : 2 * TOK] = dv_ref[span].astype(BF)
        f_ref[i, 2 * TOK : 2 * TOK + SHARD] = jnp.zeros((SHARD, FEAT), BF)


def sum_first(e_ref, f_in, dq_ref, f_ref, shard_ref, sem):
    del f_in
    total = e_ref[0].astype(F32)
    for i in range(1, SIDE):
        total = total + e_ref[i].astype(F32)
    shards = total[:STRIP].astype(BF)
    for i in range(SIDE):
        shard_ref[i] = shards[i * SHARD : (i + 1) * SHARD]
    copy = pltpu.make_async_copy(shard_ref, f_ref.at[:, 2 * TOK : 2 * TOK + SHARD], sem)
    copy.start()
    dq_ref[...] = (total[STRIP:].T * HD ** (-0.5)).astype(BF)
    copy.wait()


def sum_second(f_ref, dk_ref, dv_ref, dw_ref):
    total = f_ref[0].astype(F32)
    for i in range(1, SIDE):
        total = total + f_ref[i].astype(F32)
    dk_ref[...] = total[0:TOK].astype(BF)
    dv_ref[...] = total[TOK : 2 * TOK].astype(BF)
    dw_ref[...] = total[2 * TOK : 2 * TOK + SHARD]


def finish(residual_ref, gate_ref, *refs):
    total = refs[0][...].astype(F32)
    for ref in refs[1:-1]:
        total = total + ref[...].astype(F32)
    refs[-1][...] = (residual_ref[...].astype(F32) + gate_ref[...] * total.T).astype(BF)


def local(queries, keys, values, residual, gate, w_out, grad_out, group_mask, group_of_slot):
    z = lax.axis_index(COL)
    p = lax.axis_index(ROW)
    anywhere = pl.BlockSpec(memory_space=pl.ANY)

    def scratch(rows):
        return [pltpu.VMEM((rows, FEAT), BF), pltpu.SemaphoreType.DMA((SIDE,))]

    own = whole((TOK, FEAT))
    col_spec = whole((SIDE, 2 * TOK + SHARD, FEAT))
    row_spec = whole((SIDE, STRIP + TOK, FEAT))
    sent = call(
        first_payload,
        out((SIDE, 2 * TOK + SHARD, FEAT)),
        [own, own, whole((SHARD, FEAT))],
        data=1 << 20,
    )(*hbm(keys, values, w_out.T))
    kvw = swap(sent, COL)

    slots = group_of_slot.reshape(SIDE, SIDE, TOK // GROUP)
    query_groups = lax.dynamic_index_in_dim(slots, z, 0, keepdims=False).reshape(GROUPS)
    key_groups = lax.dynamic_index_in_dim(slots, p, 1, keepdims=False).reshape(GROUPS)
    ids = jnp.arange(group_mask.shape[0], dtype=jnp.int32)
    query_hot = (query_groups[:, None] == ids[None, :]).astype(BF)
    key_hot = (key_groups[:, None] == ids[None, :]).astype(BF)
    picked = jnp.einsum(
        "qa,ab->bq", query_hot, (group_mask == 1).astype(BF), preferred_element_type=F32
    ).astype(BF)
    table = jnp.einsum("kb,bq->kq", key_hot, picked, preferred_element_type=F32)
    bias = jnp.where(table > 0.5, 0.0, MASKED).astype(BF)
    bias = jnp.broadcast_to(bias[:, :, None], (GROUPS, GROUPS, GROUP)).reshape(GROUPS, BLOCK)

    gated = (grad_out.astype(F32) * gate[None, :]).astype(BF)
    gated = gated.reshape(TOK, SIDE, SIDE, SHARD).transpose(0, 2, 1, 3).reshape(TOK, SIDE * STRIP)
    gated_t = gated.T

    sent = call(
        second_payload,
        far((SIDE, STRIP + TOK, FEAT)),
        [col_spec, own],
        data=2 << 20,
        out_specs=anywhere,
        scratch_shapes=scratch(STRIP + TOK),
    )(kvw, queries)
    wq = swap(sent, ROW)

    gated, wq, bias = lax.optimization_barrier((gated, wq, bias))
    sent = call(
        grad_payload,
        far((SIDE, FEAT, TOK)),
        [whole((TOK, SIDE * STRIP)), at((SIDE, STRIP, FEAT), (0, 0, 0))],
        flops=2 * TOK * FEAT * SIDE * STRIP,
        data=2 << 20,
        out_specs=anywhere,
        scratch_shapes=scratch(FEAT),
    )(gated, wq)
    grad_t = swap(sent, ROW)

    query_spec = at((SIDE, TOK, FEAT), (0, STRIP // TOK, 0))
    key_spec = at((SIDE, TOK, FEAT), (0, 0, 0))
    value_spec = at((SIDE, TOK, FEAT), (0, 1, 0))
    bias_spec = whole((GROUPS, BLOCK))
    stat_spec = whole((STATS, TOK))
    pair_count = HEADS_HERE * BLOCK * BLOCK
    half_spec = whole((FEAT, BLOCK))
    part, mean_key, part_lse = call(
        forward,
        (out((FEAT, BLOCK)), out((FEAT, BLOCK)), out((STATS, TOK), F32)),
        [query_spec, key_spec, value_spec, bias_spec],
        flops=24 * HD * pair_count,
        data=2 << 20,
        exps=pair_count,
    )(wq, kvw, kvw, bias)
    sent, part_delta = call(
        stats_payload,
        (far((SIDE, FEAT + 6 * STATS, TOK)), out((STATS, TOK), F32)),
        [half_spec, stat_spec, whole((SIDE, FEAT, TOK))],
        data=2 << 20,
    )(part, part_lse, grad_t)
    parts = swap(sent, ROW)
    block_specs = [
        query_spec,
        key_spec,
        value_spec,
        whole((SIDE, FEAT, TOK)),
        bias_spec,
        stat_spec,
        stat_spec,
    ]
    query_share = call(
        query_grad,
        out((FEAT, BLOCK)),
        block_specs,
        flops=24 * HD * pair_count,
        data=3 << 20,
        exps=pair_count,
    )(wq, kvw, kvw, grad_t, bias, part_lse, part_delta)

    parts, query_share = lax.optimization_barrier((parts, query_share))
    lse, delta, attended = call(
        combine,
        (out((STATS, TOK), F32), out((STATS, TOK), F32), out((TOK, FEAT))),
        [pl.BlockSpec(memory_space=pltpu.SMEM), whole((SIDE, FEAT + 6 * STATS, TOK))],
        data=1 << 20,
        scratch_shapes=[pltpu.VMEM((SIDE, STATS, TOK), F32)],
    )(p.reshape(1).astype(jnp.int32), parts)
    scalar = pl.BlockSpec(memory_space=pltpu.SMEM)
    place = jnp.stack([lax.axis_index("yh"), lax.axis_index("core")]).astype(jnp.int32)
    keep, send = call(
        branch_rows,
        (out((PAIRS, STRIP, TOK)), out((PAIRS, STRIP, TOK))),
        [scalar, own, at((SIDE, STRIP, FEAT), (0, 0, 0))],
        flops=2 * TOK * FEAT * SIDE * STRIP,
        data=2 << 20,
        scratch_shapes=[pltpu.VMEM((SIDE, STRIP, TOK), BF)],
    )(place, attended, wq)
    got = lax.ppermute(send, "core", [(0, 1), (1, 0)])
    chunks = call(
        add_halves,
        (out((STRIP, TOK)),) * PAIRS,
        [scalar] + [whole((PAIRS, STRIP, TOK))] * 2,
        data=2 << 20,
    )(place, keep, got)

    sent_row = call(
        row_payload,
        far((SIDE, STRIP + TOK, FEAT)),
        [half_spec, half_spec] + [stat_spec] * 4 + [own, whole((SIDE * STRIP, TOK))],
        flops=2 * TOK * FEAT * SIDE * STRIP,
        data=3 << 20,
        out_specs=anywhere,
        scratch_shapes=[
            pltpu.VMEM((SIDE, STRIP + TOK, FEAT), BF),
            pltpu.SemaphoreType.DMA((SIDE,)),
        ],
    )(query_share, mean_key, part_lse, part_delta, lse, delta, attended, gated_t)
    got_row = swap(sent_row, ROW)
    got_row, chunks = lax.optimization_barrier((got_row, chunks))
    mine, far_chunk, ahead_chunk, behind_chunk = chunks

    def pass_on(a, step):
        pairs = [
            (2 * i + c, 2 * ((i + step * (1 - 2 * c)) % PAIRS) + c)
            for i in range(PAIRS)
            for c in range(2)
        ]
        return lax.ppermute(a, FSDP, pairs)

    strip_spec = whole((STRIP, TOK))
    from_ahead = pass_on(behind_chunk, -1)
    ahead_chunk = call(relay, out((STRIP, TOK)), [strip_spec, strip_spec], data=1 << 18)(
        ahead_chunk, pass_on(far_chunk, 1)
    )
    summed = (mine, from_ahead, pass_on(ahead_chunk, 1))
    col_shape = (SIDE, 2 * TOK + SHARD, FEAT)
    sent_col = call(
        key_grads,
        far(col_shape),
        block_specs,
        flops=32 * HD * pair_count,
        data=3 << 20,
        exps=pair_count,
        scratch_shapes=[pltpu.VMEM((BLOCK, FEAT), F32)] * 2,
    )(wq, kvw, kvw, grad_t, bias, lse, delta)
    d_queries, sent_col = call(
        sum_first,
        (out((TOK, FEAT)), far(col_shape)),
        [row_spec, anywhere],
        data=2 << 20,
        out_specs=(own, anywhere),
        input_output_aliases={1: 1},
        scratch_shapes=[pltpu.VMEM((SIDE, SHARD, FEAT), BF), pltpu.SemaphoreType.DMA],
    )(got_row, sent_col)
    got_col = swap(sent_col, COL)
    d_keys, d_values, d_weight = call(
        sum_second,
        (out((TOK, FEAT)), out((TOK, FEAT)), out((SHARD, FEAT), F32)),
        [col_spec],
        data=1 << 20,
    )(got_col)

    col_count = residual.shape[1]
    gate_here = lax.dynamic_slice_in_dim(gate, lax.axis_index(FSDP) * col_count, col_count, 0)
    layer_out = call(
        finish,
        out((TOK, STRIP)),
        [whole((TOK, STRIP)), whole((1, STRIP))] + [strip_spec] * 3,
        data=1 << 20,
    )(residual, gate_here[None, :], *summed)
    return (layer_out, d_queries, d_keys, d_values, d_weight.T)


def solution(mesh):
    fine = Mesh(mesh.devices.reshape(8, 4, 2, 4, 2), ("z", "x", "yl", "yh", "core"))
    seq = COL + ROW
    tile = P(seq, FSDP)
    in_specs = (tile, tile, tile, tile, P(), P(FSDP, seq), P(seq, None), P(), P())
    out_specs = (tile, tile, tile, tile, P(FSDP, seq))
    return jax.shard_map(local, mesh=fine, in_specs=in_specs, out_specs=out_specs, check_vma=False)
```

```python
import jax
import jax.numpy as jnp
from jax import lax
from jax.experimental import pallas as pl
from jax.experimental.pallas import tpu as pltpu
from jax.sharding import Mesh, PartitionSpec as P

ROW = ("x", "yl")
COL = ("z",)
FSDP = ("yh", "core")
SIDE = 8
PAIRS = 4
TOK = 128
BLOCK = SIDE * TOK
FEAT = 128
HEADS_HERE = 2
HD = 64
GROUP = 64
GROUPS = BLOCK // GROUP
SHARD = 48
STRIP = SIDE * SHARD
QUERY_TILE = 512
KEY_TILE = 256
MASKED = -1e30
STATS = HEADS_HERE * SIDE
VMEM = 32 * 1024 * 1024
BF = jnp.bfloat16
F32 = jnp.float32


def mm(a, b):
    return jnp.dot(a, b, preferred_element_type=F32)


def call(body, out_shape, in_specs, flops=1, data=1, exps=0, out_specs=None, grid=(1,), **kw):
    if out_specs is None:
        out_specs = jax.tree.map(lambda s: whole(s.shape), out_shape)
    return pl.pallas_call(
        body,
        grid=grid,
        in_specs=in_specs,
        out_specs=out_specs,
        out_shape=out_shape,
        compiler_params=pltpu.CompilerParams(vmem_limit_bytes=VMEM),
        cost_estimate=pl.CostEstimate(flops=flops, bytes_accessed=data, transcendentals=exps),
        **kw,
    )


def hbm(*arrays):
    return [pltpu.with_memory_space_constraint(a, pltpu.HBM) for a in arrays]


def whole(shape):
    return pl.BlockSpec(shape, lambda i: (0,) * len(shape))


def at(shape, index):
    return pl.BlockSpec(shape, lambda i: index)


def out(shape, dtype=BF):
    return jax.ShapeDtypeStruct(shape, dtype)


def far(shape, dtype=BF):
    return pltpu.HBM(shape, dtype)


def swap(a, axes):
    return lax.all_to_all(a, axes, 0, 0, tiled=True)


def repeat(block_ref, o_ref, sems):
    copies = [pltpu.make_async_copy(block_ref, o_ref.at[i], sems.at[i]) for i in range(SIDE)]
    for copy in copies:
        copy.start()
    for copy in copies:
        copy.wait()


def first_payload(k_ref, v_ref, w_ref, o_ref):
    for i in range(SIDE):
        o_ref[i, 0:TOK] = k_ref[...]
        o_ref[i, TOK : 2 * TOK] = v_ref[...]
        o_ref[i, 2 * TOK : 2 * TOK + SHARD] = w_ref[...]


def second_payload(g_ref, q_ref, o_ref, block_ref, sems):
    for j in range(SIDE):
        block_ref[j * SHARD : (j + 1) * SHARD] = g_ref[j, 2 * TOK : 2 * TOK + SHARD]
    block_ref[STRIP : STRIP + TOK] = q_ref[...]
    repeat(block_ref, o_ref, sems)


def grad_payload(gated_ref, w_ref, o_ref, block_ref, sems):
    total = jnp.zeros((TOK, FEAT), F32)
    for i in range(SIDE):
        total = total + mm(gated_ref[:, i * STRIP : (i + 1) * STRIP], w_ref[i])
    block_ref[...] = total.T.astype(BF)
    repeat(block_ref, o_ref, sems)


def key_operand(k):
    row = lax.broadcasted_iota(jnp.int32, (BLOCK, GROUPS), 0) // GROUP
    col = lax.broadcasted_iota(jnp.int32, (BLOCK, GROUPS), 1)
    return jnp.concatenate([k, (row == col).astype(F32).astype(BF)], axis=1)


def query_operand(q_t, bias, head):
    mine = lax.broadcasted_iota(jnp.int32, (FEAT, 1), 0) // HD == head
    part = jnp.where(mine, q_t.astype(F32) * HD ** (-0.5), 0.0).astype(BF)
    return jnp.concatenate([part, bias], axis=0)


def transposed(a):
    return a.astype(F32).T.astype(BF)


def row_of(ref, head, first=0, count=SIDE):
    rows = range(head * SIDE + first, head * SIDE + first + count)
    return jnp.concatenate([ref[i : i + 1, :] for i in rows], axis=1)


def forward(q_ref, k_ref, v_ref, bias_ref, o_ref, mean_ref, lse_ref):
    q_t = transposed(q_ref[...].reshape(BLOCK, FEAT))
    k = k_ref[...].reshape(BLOCK, FEAT)
    k_op = key_operand(k)
    k_t = transposed(k)
    v_t = transposed(v_ref[...].reshape(BLOCK, FEAT))
    for head in range(HEADS_HERE):
        rows = slice(head * HD, (head + 1) * HD)
        s = mm(k_op, query_operand(q_t, bias_ref[...], head))
        top = jnp.max(s, axis=0, keepdims=True)
        p = jnp.exp(s - top)
        total = jnp.sum(p, axis=0, keepdims=True)
        both = jnp.concatenate([v_t[rows], k_t[rows]], axis=0)
        part = mm(both, p.astype(BF)) * (1.0 / total)
        o_ref[rows] = part[:HD].astype(BF)
        mean_ref[rows] = part[HD:].astype(BF)
        lse = top + jnp.log(total)
        for c in range(SIDE):
            row = head * SIDE + c
            lse_ref[row : row + 1, :] = lse[:, c * TOK : (c + 1) * TOK]


def split3(a):
    hi = a.astype(BF)
    rest = a - hi.astype(F32)
    mid = rest.astype(BF)
    return hi, mid, (rest - mid.astype(F32)).astype(BF)


def stats_payload(o_ref, lse_ref, grad_ref, out_ref, delta_ref):
    for c in range(SIDE):
        part = o_ref[:, c * TOK : (c + 1) * TOK]
        product = part.astype(F32) * grad_ref[c].astype(F32)
        for head in range(HEADS_HERE):
            row = head * SIDE + c
            delta_ref[row : row + 1, :] = jnp.sum(
                product[head * HD : (head + 1) * HD], axis=0, keepdims=True
            )
        out_ref[c, 0:FEAT] = part
    pieces = jnp.concatenate(split3(lse_ref[...]) + split3(delta_ref[...]), axis=0)
    for c in range(SIDE):
        out_ref[c, FEAT : FEAT + 6 * STATS] = pieces


def query_grad(q_ref, k_ref, v_ref, grad_ref, bias_ref, lse_ref, delta_ref, o_ref):
    k = k_ref[...].reshape(BLOCK, FEAT)
    v = v_ref[...].reshape(BLOCK, FEAT)
    q_t = transposed(q_ref[...].reshape(BLOCK, FEAT))
    k_t = transposed(k)
    k_op = key_operand(k)
    grad_t = jnp.concatenate([grad_ref[c] for c in range(SIDE)], axis=1)
    feat_row = lax.broadcasted_iota(jnp.int32, (FEAT, 1), 0) // HD
    for head in range(HEADS_HERE):
        rows = slice(head * HD, (head + 1) * HD)
        q_op = query_operand(q_t, bias_ref[...], head)
        grad_op = jnp.where(feat_row == head, grad_t.astype(F32), 0.0).astype(BF)
        for tile in range(BLOCK // QUERY_TILE):
            span = slice(tile * QUERY_TILE, (tile + 1) * QUERY_TILE)
            part = (head, tile * (QUERY_TILE // TOK), QUERY_TILE // TOK)
            p = jnp.exp(mm(k_op, q_op[:, span]) - row_of(lse_ref, *part))
            ds = (p * (mm(v, grad_op[:, span]) - row_of(delta_ref, *part))).astype(BF)
            o_ref[rows, span] = mm(k_t[rows], ds).astype(BF)


def combine(me_ref, d_ref, lse_ref, delta_ref, att_ref, weight_ref):
    def quantity(j, first):
        at_row = FEAT + first * STATS
        return sum(
            d_ref[j, at_row + i * STATS : at_row + (i + 1) * STATS].astype(F32) for i in range(3)
        )

    lse = [quantity(j, 0) for j in range(SIDE)]
    top = lse[0]
    for j in range(1, SIDE):
        top = jnp.maximum(top, lse[j])
    total = jnp.zeros_like(top)
    for j in range(SIDE):
        total = total + jnp.exp(lse[j] - top)
    all_lse = top + jnp.log(total)
    lse_ref[...] = all_lse
    delta = jnp.zeros_like(top)
    for j in range(SIDE):
        weight = jnp.exp(lse[j] - all_lse)
        weight_ref[j] = weight
        delta = delta + weight * quantity(j, 3)
    delta_ref[...] = delta
    me = me_ref[0]
    heads = []
    for head in range(HEADS_HERE):
        acc = jnp.zeros((HD, TOK), F32)
        for j in range(SIDE):
            weight = weight_ref[j, pl.ds(head * SIDE + me, 1), :]
            acc = acc + weight * d_ref[j, head * HD : (head + 1) * HD].astype(F32)
        heads.append(acc)
    att_ref[...] = jnp.concatenate(heads, axis=0).T.astype(BF)


def branch_rows(core_ref, att_ref, w_ref, keep_ref, send_ref, all_ref):
    att = att_ref[...]
    for i in range(SIDE):
        part = lax.dot_general(
            w_ref[i], att, (((1,), (1,)), ((), ())), preferred_element_type=F32
        ).astype(BF)
        for j in range(SIDE):
            all_ref[j, i * SHARD : (i + 1) * SHARD] = part[j * SHARD : (j + 1) * SHARD]
    core = core_ref[0]
    for i in range(PAIRS):
        keep_ref[i] = all_ref[2 * i + core]
        send_ref[i] = all_ref[2 * i + 1 - core]


def add_halves(pair_ref, core_ref, keep_ref, got_ref, own_ref, far_ref, ahead_ref, behind_ref):
    pair, ahead = pair_ref[0], 1 - 2 * core_ref[0]
    steps = ((own_ref, 0), (far_ref, 2), (ahead_ref, ahead), (behind_ref, -ahead))
    for ref, step in steps:
        i = lax.rem(pair + step + PAIRS, PAIRS)
        ref[...] = (keep_ref[i].astype(F32) + got_ref[i].astype(F32)).astype(BF)


def relay(ahead_ref, got_ref, o_ref):
    o_ref[...] = (ahead_ref[...].astype(F32) + got_ref[...].astype(F32)).astype(BF)


def row_payload(
    grad_ref, mean_ref, lse_ref, delta_ref, all_lse_ref, all_delta_ref, att_ref, gated_ref, o_ref,
    e_ref, sems,
):
    att = att_ref[...]
    copies = []
    for i in range(SIDE):
        cols = slice(i * TOK, (i + 1) * TOK)
        for head in range(HEADS_HERE):
            rows = slice(head * HD, (head + 1) * HD)
            row = slice(head * SIDE + i, head * SIDE + i + 1)
            weight = jnp.exp(lse_ref[row, :] - all_lse_ref[row, :])
            shift = all_delta_ref[row, :] - delta_ref[row, :]
            part = grad_ref[rows, cols].astype(F32) - shift * mean_ref[rows, cols].astype(F32)
            e_ref[i, STRIP + head * HD : STRIP + (head + 1) * HD] = (weight * part).astype(BF)
        e_ref[i, 0:STRIP] = mm(gated_ref[i * STRIP : (i + 1) * STRIP], att).astype(BF)
        copies.append(pltpu.make_async_copy(e_ref.at[i], o_ref.at[i], sems.at[i]))
        copies[i].start()
    for copy in copies:
        copy.wait()


def key_grads(
    q_ref, k_ref, v_ref, grad_ref, bias_ref, lse_ref, delta_ref, f_ref, dk_ref, dv_ref
):
    q = q_ref[...].reshape(BLOCK, FEAT)
    k = k_ref[...].reshape(BLOCK, FEAT)
    v = v_ref[...].reshape(BLOCK, FEAT)
    q_t = transposed(q)
    k_op = key_operand(k)
    grad_t = jnp.concatenate([grad_ref[c] for c in range(SIDE)], axis=1)
    grad = transposed(grad_t)
    feat_row = lax.broadcasted_iota(jnp.int32, (FEAT, 1), 0) // HD
    feat_col = lax.broadcasted_iota(jnp.int32, (1, FEAT), 1) // HD
    dk_ref[...] = jnp.zeros_like(dk_ref)
    dv_ref[...] = jnp.zeros_like(dv_ref)
    for head in range(HEADS_HERE):
        q_op = query_operand(q_t, bias_ref[...], head)
        grad_op = jnp.where(feat_row == head, grad_t.astype(F32), 0.0).astype(BF)
        q_rows = jnp.where(feat_col == head, q.astype(F32), 0.0).astype(BF)
        grad_rows = jnp.where(feat_col == head, grad.astype(F32), 0.0).astype(BF)
        for tile in range(BLOCK // KEY_TILE):
            span = slice(tile * KEY_TILE, (tile + 1) * KEY_TILE)
            part = (head, tile * (KEY_TILE // TOK), KEY_TILE // TOK)
            p = jnp.exp(mm(k_op, q_op[:, span]) - row_of(lse_ref, *part))
            ds = (p * (mm(v, grad_op[:, span]) - row_of(delta_ref, *part))).astype(BF)
            dv_ref[...] += mm(p.astype(BF), grad_rows[span])
            dk_ref[...] += mm(ds, q_rows[span])
    for i in range(SIDE):
        span = slice(i * TOK, (i + 1) * TOK)
        f_ref[i, 0:TOK] = (dk_ref[span] * HD ** (-0.5)).astype(BF)
        f_ref[i, TOK : 2 * TOK] = dv_ref[span].astype(BF)
        f_ref[i, 2 * TOK : 2 * TOK + SHARD] = jnp.zeros((SHARD, FEAT), BF)


def sum_first(e_ref, f_in, dq_ref, f_ref, shard_ref, sem):
    del f_in
    total = e_ref[0].astype(F32)
    for i in range(1, SIDE):
        total = total + e_ref[i].astype(F32)
    shards = total[:STRIP].astype(BF)
    for i in range(SIDE):
        shard_ref[i] = shards[i * SHARD : (i + 1) * SHARD]
    copy = pltpu.make_async_copy(shard_ref, f_ref.at[:, 2 * TOK : 2 * TOK + SHARD], sem)
    copy.start()
    dq_ref[...] = (total[STRIP:].T * HD ** (-0.5)).astype(BF)
    copy.wait()


def sum_second(f_ref, dk_ref, dv_ref, dw_ref):
    total = f_ref[0].astype(F32)
    for i in range(1, SIDE):
        total = total + f_ref[i].astype(F32)
    dk_ref[...] = total[0:TOK].astype(BF)
    dv_ref[...] = total[TOK : 2 * TOK].astype(BF)
    dw_ref[...] = total[2 * TOK : 2 * TOK + SHARD]


def finish(residual_ref, gate_ref, *refs):
    total = refs[0][...].astype(F32)
    for ref in refs[1:-1]:
        total = total + ref[...].astype(F32)
    refs[-1][...] = (residual_ref[...].astype(F32) + gate_ref[...] * total.T).astype(BF)


def local(queries, keys, values, residual, gate, w_out, grad_out, group_mask, group_of_slot):
    z = lax.axis_index(COL)
    p = lax.axis_index(ROW)
    anywhere = pl.BlockSpec(memory_space=pl.ANY)

    def scratch(rows):
        return [pltpu.VMEM((rows, FEAT), BF), pltpu.SemaphoreType.DMA((SIDE,))]

    own = whole((TOK, FEAT))
    col_spec = whole((SIDE, 2 * TOK + SHARD, FEAT))
    row_spec = whole((SIDE, STRIP + TOK, FEAT))
    sent = call(
        first_payload,
        out((SIDE, 2 * TOK + SHARD, FEAT)),
        [own, own, whole((SHARD, FEAT))],
        data=1 << 20,
    )(*hbm(keys, values, w_out.T))
    kvw = swap(sent, COL)

    slots = group_of_slot.reshape(SIDE, SIDE, TOK // GROUP)
    query_groups = lax.dynamic_index_in_dim(slots, z, 0, keepdims=False).reshape(GROUPS)
    key_groups = lax.dynamic_index_in_dim(slots, p, 1, keepdims=False).reshape(GROUPS)
    ids = jnp.arange(group_mask.shape[0], dtype=jnp.int32)
    query_hot = (query_groups[:, None] == ids[None, :]).astype(BF)
    key_hot = (key_groups[:, None] == ids[None, :]).astype(BF)
    picked = jnp.einsum(
        "qa,ab->bq", query_hot, (group_mask == 1).astype(BF), preferred_element_type=F32
    ).astype(BF)
    table = jnp.einsum("kb,bq->kq", key_hot, picked, preferred_element_type=F32)
    bias = jnp.where(table > 0.5, 0.0, MASKED).astype(BF)
    bias = jnp.broadcast_to(bias[:, :, None], (GROUPS, GROUPS, GROUP)).reshape(GROUPS, BLOCK)

    gated = (grad_out.astype(F32) * gate[None, :]).astype(BF)
    gated = gated.reshape(TOK, SIDE, SIDE, SHARD).transpose(0, 2, 1, 3).reshape(TOK, SIDE * STRIP)
    gated_t = gated.T

    sent = call(
        second_payload,
        far((SIDE, STRIP + TOK, FEAT)),
        [col_spec, own],
        data=2 << 20,
        out_specs=anywhere,
        scratch_shapes=scratch(STRIP + TOK),
    )(kvw, queries)
    wq = swap(sent, ROW)

    gated, wq, bias = lax.optimization_barrier((gated, wq, bias))
    sent = call(
        grad_payload,
        far((SIDE, FEAT, TOK)),
        [whole((TOK, SIDE * STRIP)), at((SIDE, STRIP, FEAT), (0, 0, 0))],
        flops=2 * TOK * FEAT * SIDE * STRIP,
        data=2 << 20,
        out_specs=anywhere,
        scratch_shapes=scratch(FEAT),
    )(gated, wq)
    grad_t = swap(sent, ROW)

    query_spec = at((SIDE, TOK, FEAT), (0, STRIP // TOK, 0))
    key_spec = at((SIDE, TOK, FEAT), (0, 0, 0))
    value_spec = at((SIDE, TOK, FEAT), (0, 1, 0))
    bias_spec = whole((GROUPS, BLOCK))
    stat_spec = whole((STATS, TOK))
    pair_count = HEADS_HERE * BLOCK * BLOCK
    half_spec = whole((FEAT, BLOCK))
    part, mean_key, part_lse = call(
        forward,
        (out((FEAT, BLOCK)), out((FEAT, BLOCK)), out((STATS, TOK), F32)),
        [query_spec, key_spec, value_spec, bias_spec],
        flops=24 * HD * pair_count,
        data=2 << 20,
        exps=pair_count,
    )(wq, kvw, kvw, bias)
    sent, part_delta = call(
        stats_payload,
        (far((SIDE, FEAT + 6 * STATS, TOK)), out((STATS, TOK), F32)),
        [half_spec, stat_spec, whole((SIDE, FEAT, TOK))],
        data=2 << 20,
    )(part, part_lse, grad_t)
    parts = swap(sent, ROW)
    block_specs = [
        query_spec,
        key_spec,
        value_spec,
        whole((SIDE, FEAT, TOK)),
        bias_spec,
        stat_spec,
        stat_spec,
    ]
    query_share = call(
        query_grad,
        out((FEAT, BLOCK)),
        block_specs,
        flops=24 * HD * pair_count,
        data=3 << 20,
        exps=pair_count,
    )(wq, kvw, kvw, grad_t, bias, part_lse, part_delta)

    parts, query_share = lax.optimization_barrier((parts, query_share))
    lse, delta, attended = call(
        combine,
        (out((STATS, TOK), F32), out((STATS, TOK), F32), out((TOK, FEAT))),
        [pl.BlockSpec(memory_space=pltpu.SMEM), whole((SIDE, FEAT + 6 * STATS, TOK))],
        data=1 << 20,
        scratch_shapes=[pltpu.VMEM((SIDE, STATS, TOK), F32)],
    )(p.reshape(1).astype(jnp.int32), parts)
    scalar = pl.BlockSpec(memory_space=pltpu.SMEM)
    core = lax.axis_index("core").reshape(1).astype(jnp.int32)
    pair = lax.axis_index("yh").reshape(1).astype(jnp.int32)
    keep, send = call(
        branch_rows,
        (out((PAIRS, STRIP, TOK)), out((PAIRS, STRIP, TOK))),
        [scalar, own, at((SIDE, STRIP, FEAT), (0, 0, 0))],
        flops=2 * TOK * FEAT * SIDE * STRIP,
        data=2 << 20,
        scratch_shapes=[pltpu.VMEM((SIDE, STRIP, TOK), BF)],
    )(core, attended, wq)
    got = lax.ppermute(send, "core", [(0, 1), (1, 0)])
    chunks = call(
        add_halves,
        (out((STRIP, TOK)),) * PAIRS,
        [scalar] * 2 + [whole((PAIRS, STRIP, TOK))] * 2,
        data=2 << 20,
    )(pair, core, keep, got)

    sent_row = call(
        row_payload,
        far((SIDE, STRIP + TOK, FEAT)),
        [half_spec, half_spec] + [stat_spec] * 4 + [own, whole((SIDE * STRIP, TOK))],
        flops=2 * TOK * FEAT * SIDE * STRIP,
        data=3 << 20,
        out_specs=anywhere,
        scratch_shapes=[
            pltpu.VMEM((SIDE, STRIP + TOK, FEAT), BF),
            pltpu.SemaphoreType.DMA((SIDE,)),
        ],
    )(query_share, mean_key, part_lse, part_delta, lse, delta, attended, gated_t)
    got_row = swap(sent_row, ROW)
    got_row, chunks = lax.optimization_barrier((got_row, chunks))
    mine, far_chunk, ahead_chunk, behind_chunk = chunks

    def pass_on(a, step):
        pairs = [
            (2 * i + c, 2 * ((i + step * (1 - 2 * c)) % PAIRS) + c)
            for i in range(PAIRS)
            for c in range(2)
        ]
        return lax.ppermute(a, FSDP, pairs)

    strip_spec = whole((STRIP, TOK))
    from_ahead = pass_on(behind_chunk, -1)
    ahead_chunk = call(relay, out((STRIP, TOK)), [strip_spec, strip_spec], data=1 << 18)(
        ahead_chunk, pass_on(far_chunk, 1)
    )
    summed = (mine, from_ahead, pass_on(ahead_chunk, 1))
    col_shape = (SIDE, 2 * TOK + SHARD, FEAT)
    sent_col = call(
        key_grads,
        far(col_shape),
        block_specs,
        flops=32 * HD * pair_count,
        data=3 << 20,
        exps=pair_count,
        scratch_shapes=[pltpu.VMEM((BLOCK, FEAT), F32)] * 2,
    )(wq, kvw, kvw, grad_t, bias, lse, delta)
    d_queries, sent_col = call(
        sum_first,
        (out((TOK, FEAT)), far(col_shape)),
        [row_spec, anywhere],
        data=2 << 20,
        out_specs=(own, anywhere),
        input_output_aliases={1: 1},
        scratch_shapes=[pltpu.VMEM((SIDE, SHARD, FEAT), BF), pltpu.SemaphoreType.DMA],
    )(got_row, sent_col)
    got_col = swap(sent_col, COL)
    d_keys, d_values, d_weight = call(
        sum_second,
        (out((TOK, FEAT)), out((TOK, FEAT)), out((SHARD, FEAT), F32)),
        [col_spec],
        data=1 << 20,
    )(got_col)

    col_count = residual.shape[1]
    gate_here = lax.dynamic_slice_in_dim(gate, lax.axis_index(FSDP) * col_count, col_count, 0)
    layer_out = call(
        finish,
        out((TOK, STRIP)),
        [whole((TOK, STRIP)), whole((1, STRIP))] + [strip_spec] * 3,
        data=1 << 20,
    )(residual, gate_here[None, :], *summed)
    return (layer_out, d_queries, d_keys, d_values, d_weight.T)


def solution(mesh):
    fine = Mesh(mesh.devices.reshape(8, 4, 2, 4, 2), ("z", "x", "yl", "yh", "core"))
    seq = COL + ROW
    tile = P(seq, FSDP)
    in_specs = (tile, tile, tile, tile, P(), P(FSDP, seq), P(seq, None), P(), P())
    out_specs = (tile, tile, tile, tile, P(FSDP, seq))
    return jax.shard_map(local, mesh=fine, in_specs=in_specs, out_specs=out_specs, check_vma=False)
```
